128 devices in a mesh: rows: 4 (over y), cols: 32 (over z, x, core).
Axes of the slice: x: 4, y: 4, z: 4, core: 2. Of those that a mesh axis runs over, the one named last changes fastest.
Arguments:
- pixels: bfloat16 [128, 1024, 768], P('rows', 'cols'), may hold values from -6 to 6
- tissue: int32 [128, 1024], P('rows', 'cols'), may hold values 0 or 1
- patch_weight: bfloat16 [768, 1024], replicated, may hold values from -0.21875 to 0.21875
- conv_weight: bfloat16 [9, 32, 1024], replicated, may hold values from -0.375 to 0.375
- kv_weight: bfloat16 [1024, 2048], replicated, may hold values from -0.1875 to 0.1875
- query_weight: bfloat16 [1024, 1024], replicated, may hold values from -0.1875 to 0.1875
- out_weight: bfloat16 [1024, 1024], replicated, may hold values from -0.1875 to 0.1875
- latents: bfloat16 [512, 1024], replicated, may hold values from -240 to 240
Outputs:
- features: bfloat16 [128, 1024, 1024], P('rows', 'cols')
- latents_out: bfloat16 [512, 1024], P(('rows', 'cols'))
The draws below stay inside these ranges and needn't reach their ends.
Inputs may be any that keep to these rules, and one draw needn't show every extreme that they name: 1 marks a patch tile that holds tissue, and at least one tile of the slab holds tissue.
All inputs are finite; a program needn't handle non-finite values. No bound on the sum of `tissue` on one device may be relied on, other than what follows from the above.
Results may differ from the reference program's by a relative error of at most 0.03.
Values may be sent and summed in bfloat16 or wider, within the bound.
No kernel may reach another device: no remote copies, remote signals or barrier semaphores. Data moves between devices by JAX's collectives and lax.ppermute only.
A program may use at most 128 MiB of HBM per device.

```python
import jax
import jax.numpy as jnp
from jax import lax

D = 1024
HEADS = 16
LAT = 512
PATCH_IN = 768
NR = 128
NC = 1024
GW = 32


def draw_latents(key, part):
    first_key = jax.random.fold_in(key, 0)
    drawn = jax.random.normal(first_key, (LAT, D), jnp.float32)
    drawn = jnp.clip(drawn, -6.0, 6.0)
    return drawn.astype(jnp.bfloat16)


def touch_ends(values, own_key, smallest, high):
    extent = values.shape
    index_at = [jax.random.randint(jax.random.fold_in(own_key, axis), (), 0, extent[axis]) for axis in range(len(extent))]
    values = values.at[tuple(index_at)].set(smallest)
    longest = extent.index(max(extent))
    index_at[longest] = (index_at[longest] + 1) % extent[longest]
    return values.at[tuple(index_at)].set(high)


def block_scale(stream_key, dims, cuts, least, largest):
    gain = 1.0
    for position, blocks in cuts:
        steps = jax.random.uniform(jax.random.fold_in(jax.random.fold_in(stream_key, 6), position), (blocks,), jnp.float32, least / len(cuts), largest / len(cuts))
        gain = gain * jnp.repeat(jnp.exp(steps), dims[position] // blocks).reshape((-1,) + (1,) * (len(dims) - 1 - position))
    return gain


def gaussian(rng, extent, width, bound, pieces=(), kind=jnp.bfloat16):
    result = jax.random.normal(rng, extent, jnp.float32) * width
    if len(pieces) > 0:
        result = block_scale(rng, extent, pieces, -0.22, 0.18) * result
    return jnp.clip(result, min=-bound, max=bound).astype(kind)


def setup_inputs(seed: int = 0) -> dict:
    key_of = jax.random.split(jax.random.key(seed), 9)
    pixels = gaussian(key_of[0], (NR, NC, PATCH_IN), 1.0, 6.0, ((0, 4), (1, 32)))
    tissue = touch_ends((jax.random.randint(key_of[1], (NR, NC), 0, 5) < 3).astype(jnp.int32), jax.random.fold_in(key_of[1], 1), 0, 1)
    patch_weight = gaussian(key_of[2], (PATCH_IN, D), PATCH_IN ** -0.5, 0.21875)
    conv_weight = gaussian(key_of[3], (9, GW, D), (9 * GW) ** -0.5, 0.375)
    kv_weight = gaussian(key_of[4], (D, 2 * D), D ** -0.5, 0.1875)
    query_weight = gaussian(key_of[5], (D, D), D ** -0.5, 0.1875)
    out_weight = gaussian(key_of[6], (D, D), D ** -0.5, 0.1875)
    latents = draw_latents(jax.random.fold_in(key_of[8], 71), 0)
    return dict(pixels=pixels, tissue=tissue, patch_weight=patch_weight, conv_weight=conv_weight, kv_weight=kv_weight, query_weight=query_weight, out_weight=out_weight, latents=latents)


def reference(pixels, tissue, patch_weight, conv_weight, kv_weight, query_weight, out_weight, latents):
    rows_all, cols_all, patch_in = pixels.shape
    channels = patch_weight.shape[1]
    token_count = rows_all * cols_all
    embedded = jnp.dot(pixels.reshape(token_count, patch_in), patch_weight, preferred_element_type=jnp.float32)
    embedded = embedded.astype(jnp.bfloat16).reshape(rows_all, cols_all, channels)
    padded = jnp.pad(embedded, ((1, 1), (1, 1), (0, 0)))
    group_width = conv_weight.shape[1]
    group_count = channels // group_width
    kernel = conv_weight.astype(jnp.float32).reshape(9, group_width, group_count, group_width)
    convolved = jnp.zeros((rows_all, cols_all, group_count, group_width), jnp.float32)
    for row_shift in range(3):
        for col_shift in range(3):
            window = padded[row_shift:row_shift + rows_all, col_shift:col_shift + cols_all]
            window = window.astype(jnp.float32).reshape(rows_all, cols_all, group_count, group_width)
            convolved = convolved + jnp.einsum('hwgi,igo->hwgo', window, kernel[3 * row_shift + col_shift])
    summed = embedded.astype(jnp.float32) + convolved.reshape(rows_all, cols_all, channels)
    average = lax.optimization_barrier(jnp.mean(summed, axis=-1, keepdims=True))
    centred = summed - average
    variance = lax.optimization_barrier(jnp.mean(centred * centred, axis=-1, keepdims=True))
    features = (centred * lax.rsqrt(variance + 1e-05)).astype(jnp.bfloat16)
    projected = jnp.dot(features.reshape(token_count, channels), kv_weight, preferred_element_type=jnp.float32).astype(jnp.bfloat16)
    head_dim = channels // HEADS
    key_vectors = projected[:, :channels].reshape(token_count, HEADS, head_dim).transpose(1, 0, 2)
    value_vectors = projected[:, channels:].reshape(token_count, HEADS, head_dim).transpose(1, 0, 2)
    queries = jnp.dot(latents, query_weight, preferred_element_type=jnp.float32).astype(jnp.bfloat16)
    latent_count = latents.shape[0]
    queries = queries.reshape(latent_count, HEADS, head_dim).transpose(1, 0, 2)
    tissue_live = tissue.reshape(token_count) > 0

    def one_head(operands):
        query_head, key_head, value_head = operands
        scores = jnp.dot(query_head, key_head.T, preferred_element_type=jnp.float32) * head_dim ** (-0.5)
        scores = jnp.where(tissue_live[None, :], scores, -1e+30)
        highest = lax.optimization_barrier(jnp.max(scores, axis=1, keepdims=True))
        weights = jnp.where(tissue_live[None, :], jnp.exp(scores - highest), 0.0)
        denominator = lax.optimization_barrier(jnp.sum(weights, axis=1, keepdims=True))
        numerator = jnp.dot(weights.astype(jnp.bfloat16), value_head, preferred_element_type=jnp.float32)
        return numerator / denominator
    attended = lax.map(one_head, (queries, key_vectors, value_vectors))
    attended = attended.transpose(1, 0, 2).reshape(latent_count, channels)
    normed = (attended * lax.rsqrt(lax.optimization_barrier(jnp.mean(attended * attended, axis=-1, keepdims=True)) + 1e-06)).astype(jnp.bfloat16)
    latents_out = jnp.dot(normed, out_weight, preferred_element_type=jnp.float32).astype(jnp.bfloat16)
    return (features, latents_out)
```

```python
import functools

import jax
import jax.numpy as jnp
from jax import lax
from jax.experimental import pallas as pl
from jax.experimental.pallas import tpu as pltpu
from jax.sharding import PartitionSpec as P

HEADS = 16
HEAD = 64
D = 1024
TILE = 32
TOK = TILE * TILE
GW = 32
LAT = 512
OWN = 4
BLK = 256
CHUNK = 256
PART = 640
DEAD = -1e30
VMEM_BYTES = 56 * 1024 * 1024
F32 = jnp.float32
BF16 = jnp.bfloat16


def params():
    return pltpu.CompilerParams(vmem_limit_bytes=VMEM_BYTES)


def iota(shape, dim):
    return lax.broadcasted_iota(jnp.int32, shape, dim)


def embed_kernel(pixels_ref, weight_ref, here_ref, left_ref, right_ref):
    cells = jnp.dot(pixels_ref[...], weight_ref[...], preferred_element_type=F32)
    here_ref[...] = cells.astype(BF16)
    left_ref[...] = pltpu.roll(cells, 1, 0).astype(BF16)
    right_ref[...] = pltpu.roll(cells, CHUNK - 1, 0).astype(BF16)


def embed(pixels, patch_weight):
    block = pl.BlockSpec((CHUNK, D), lambda i: (i, 0))
    return pl.pallas_call(
        embed_kernel,
        grid=(TOK // CHUNK,),
        in_specs=[
            pl.BlockSpec((CHUNK, pixels.shape[1]), lambda i: (i, 0)),
            pl.BlockSpec(patch_weight.shape, lambda i: (0, 0)),
        ],
        out_specs=[block] * 3,
        out_shape=[jax.ShapeDtypeStruct((TOK, D), BF16)] * 3,
        compiler_params=params(),
        cost_estimate=pl.CostEstimate(
            flops=2 * TOK * D * pixels.shape[1], bytes_accessed=9 << 20, transcendentals=0
        ),
        name="embed",
    )(pixels, patch_weight)


def query_kernel(core_ref, latents_ref, weight_ref, out_ref):
    core = core_ref[0]
    row = iota((LAT, LAT), 0)
    half = row // (LAT // 2)
    inner = row % (LAT // 2)
    kind = jnp.where(half == 0, core, 1 - core)
    source = (inner // OWN) * (2 * OWN) + kind * OWN + inner % OWN
    pick = jnp.where(iota((LAT, LAT), 1) == source, 1.0, 0.0).astype(BF16)
    ordered = jnp.dot(pick, latents_ref[...], preferred_element_type=F32).astype(BF16)
    queries = jnp.dot(ordered, weight_ref[...], preferred_element_type=F32).astype(BF16)
    out_ref[...] = (queries.astype(F32) * HEAD ** (-0.5)).astype(BF16)


def make_queries(core, latents, query_weight):
    return pl.pallas_call(
        query_kernel,
        in_specs=[
            pl.BlockSpec(memory_space=pltpu.SMEM),
            pl.BlockSpec(memory_space=pltpu.VMEM),
            pl.BlockSpec(memory_space=pltpu.VMEM),
        ],
        out_specs=pl.BlockSpec(memory_space=pltpu.VMEM),
        out_shape=jax.ShapeDtypeStruct((LAT, D), BF16),
        compiler_params=params(),
        cost_estimate=pl.CostEstimate(
            flops=3 * LAT * D * D, bytes_accessed=4 << 20, transcendentals=0
        ),
        name="queries",
    )(core, latents, query_weight)


def split3(value):
    high = value.astype(BF16).astype(F32)
    rest = value - high
    middle = rest.astype(BF16).astype(F32)
    low = (rest - middle).astype(BF16).astype(F32)
    return high, middle, low


def main_kernel(
    top_ref,
    bottom_ref,
    west_ref,
    east_ref,
    patch_ref,
    conv_ref,
    bias_ref,
    query_ref,
    here_hbm,
    left_hbm,
    right_hbm,
    kv_hbm,
    feat_hbm,
    mine_ref,
    send_ref,
    cells,
    kv,
    blocks,
    edges,
    summed,
    feats,
    proj,
    stats,
    sems,
    feat_sems,
):
    loads = [
        pltpu.make_async_copy(hbm, cells.at[d, pl.ds(TILE, TOK)], sems.at[d])
        for d, hbm in enumerate((left_hbm, here_hbm, right_hbm))
    ]
    load_kv = pltpu.make_async_copy(kv_hbm, kv, sems.at[3])
    for load in loads:
        load.start()
    load_kv.start()

    same = iota((BLK, BLK), 0) // GW == iota((BLK, BLK), 1) // GW
    for b in range(D // BLK):
        for tap in range(9):
            rows = conv_ref[tap, :, b * BLK : (b + 1) * BLK]
            tiled = jnp.concatenate([rows] * (BLK // GW), axis=0)
            blocks[b, tap * BLK : (tap + 1) * BLK, :] = jnp.where(same, tiled, jnp.zeros_like(tiled))

    weight = patch_ref[...]
    edges[0] = jnp.dot(west_ref[...], weight, preferred_element_type=F32)
    edges[1] = jnp.dot(east_ref[...], weight, preferred_element_type=F32)
    line = iota((TILE, D), 0)
    for ref, at, corner in ((top_ref, 0, 0), (bottom_ref, TILE + TOK, TILE + 1)):
        border = jnp.dot(ref[...], weight, preferred_element_type=F32)
        west = edges[0, corner : corner + 1, :]
        east = edges[1, corner : corner + 1, :]
        cells[1, at : at + TILE, :] = border.astype(BF16)
        cells[0, at : at + TILE, :] = jnp.where(
            line == 0, west, pltpu.roll(border, 1, 0)
        ).astype(BF16)
        cells[2, at : at + TILE, :] = jnp.where(
            line == TILE - 1, east, pltpu.roll(border, TILE - 1, 0)
        ).astype(BF16)
    for load in loads:
        load.wait()
    line16 = iota((16, D), 0)

    def patch_row(r, carry):
        first = pl.ds(pl.multiple_of(TILE + r * TILE, 16), 16)
        cells[0, first, :] = jnp.where(
            line16 == 0, edges[0, pl.ds(r + 1, 1), :], cells[0, first, :].astype(F32)
        ).astype(BF16)
        last = pl.ds(pl.multiple_of(2 * TILE - 16 + r * TILE, 16), 16)
        cells[2, last, :] = jnp.where(
            line16 == 15, edges[1, pl.ds(r + 1, 1), :], cells[2, last, :].astype(F32)
        ).astype(BF16)
        return carry

    lax.fori_loop(0, TILE, patch_row, 0)
    load_kv.wait()

    def chunk_step(i, carry):
        at = pl.multiple_of(i * CHUNK, CHUNK)
        for b in range(D // BLK):
            lanes = slice(b * BLK, (b + 1) * BLK)
            taps = [
                cells[dc, pl.ds(at + dr * TILE, CHUNK), lanes] for dr in range(3) for dc in range(3)
            ]
            convolved = jnp.dot(
                jnp.concatenate(taps, axis=1), blocks[b], preferred_element_type=F32
            )
            summed[:, lanes] = convolved + taps[4].astype(F32)
        u = summed[...]
        centred = u - jnp.mean(u, axis=1, keepdims=True)
        variance = jnp.mean(centred * centred, axis=1, keepdims=True)
        normal = (centred * lax.rsqrt(variance + 1e-05)).astype(BF16)
        feats[pl.ds(at, CHUNK), :] = normal
        pltpu.make_async_copy(
            feats.at[pl.ds(at, CHUNK)], feat_hbm.at[pl.ds(at, CHUNK)], feat_sems.at[i]
        ).start()
        proj[pl.ds(at, CHUNK), :] = jnp.dot(
            normal, kv[...], preferred_element_type=F32
        ).astype(BF16)
        return carry

    lax.fori_loop(0, TOK // CHUNK, chunk_step, 0)

    half_rows = LAT // 2
    lane = iota((half_rows, 128), 1)
    unit = jnp.where(lane == 0, 1.0, 0.0).astype(BF16)
    ones = jnp.ones((TOK, 128), BF16)
    stats[...] = jnp.zeros_like(stats)
    outs = (mine_ref, send_ref)

    def pair_step(p, carry):
        half = p // 4
        inner = p % 4
        keys = proj[:, pl.ds(pl.multiple_of(p * 128, 128), 128)]
        values = proj[:, pl.ds(pl.multiple_of(D + p * 128, 128), 128)]
        keys = jnp.concatenate([keys, bias_ref[...]], axis=1)
        values = jnp.concatenate([values, ones], axis=1)
        for part in range(2):
            query = query_ref[
                part * half_rows : (part + 1) * half_rows,
                pl.ds(pl.multiple_of(p * 128, 128), 128),
            ]
            sums = []
            stat = stats[part, half]
            for a in range(2):
                own = jnp.where(lane // HEAD == a, query, jnp.zeros_like(query))
                scores = lax.dot_general(
                    jnp.concatenate([own, unit], axis=1),
                    keys,
                    (((1,), (1,)), ((), ())),
                    preferred_element_type=F32,
                )
                peak = jnp.max(scores, axis=1, keepdims=True)
                weights = jnp.exp(scores - peak).astype(BF16)
                total = jnp.dot(weights, values, preferred_element_type=F32)
                sums.append(total[:, :128])
                stat = jnp.where(
                    lane % 8 == 2 * inner + a, jnp.where(lane < 24, peak, total[:, 128:]), stat
                )
            stats[part, half] = stat
            rows = pl.ds(pl.multiple_of(half * half_rows, half_rows), half_rows)
            outs[part][rows, pl.ds(pl.multiple_of(inner * 128, 128), 128)] = jnp.where(
                lane < HEAD, sums[0], sums[1]
            ).astype(BF16)
        return carry

    lax.fori_loop(0, HEADS // 2, pair_step, 0)

    for part in range(2):
        for half in range(2):
            high, middle, low = split3(stats[part, half])
            packed = jnp.where(
                lane < 8,
                high,
                jnp.where(
                    lane < 16,
                    middle,
                    jnp.where(
                        lane < 24,
                        low,
                        jnp.where(lane < 32, high, jnp.where(lane < 40, middle, 0.0)),
                    ),
                ),
            )
            outs[part][half * half_rows : (half + 1) * half_rows, 512:640] = packed.astype(BF16)

    for i in range(TOK // CHUNK):
        pltpu.make_async_copy(
            feats.at[pl.ds(i * CHUNK, CHUNK)], feat_hbm.at[pl.ds(i * CHUNK, CHUNK)], feat_sems.at[i]
        ).wait()


def main(top, bottom, west, east, patch_weight, conv_weight, bias, queries, shifted, kv_weight):
    vmem = pl.BlockSpec(memory_space=pltpu.VMEM)
    hbm = pl.BlockSpec(memory_space=pl.ANY)
    here, left, right = shifted
    return pl.pallas_call(
        main_kernel,
        in_specs=[vmem] * 8 + [hbm] * 4,
        out_specs=[hbm, vmem, vmem],
        out_shape=[
            jax.ShapeDtypeStruct((TOK, D), BF16),
            jax.ShapeDtypeStruct((LAT, PART), BF16),
            jax.ShapeDtypeStruct((LAT, PART), BF16),
        ],
        scratch_shapes=[
            pltpu.VMEM((3, TOK + 2 * TILE, D), BF16),
            pltpu.VMEM((D, 2 * D), BF16),
            pltpu.VMEM((D // BLK, 9 * BLK, BLK), BF16),
            pltpu.VMEM((2, TILE + 2, D), F32),
            pltpu.VMEM((CHUNK, D), F32),
            pltpu.VMEM((TOK, D), BF16),
            pltpu.VMEM((TOK, 2 * D), BF16),
            pltpu.VMEM((2, 2, LAT // 2, 128), F32),
            pltpu.SemaphoreType.DMA((4,)),
            pltpu.SemaphoreType.DMA((TOK // CHUNK,)),
        ],
        compiler_params=params(),
        cost_estimate=pl.CostEstimate(
            flops=16 << 30, bytes_accessed=24 << 20, transcendentals=8 << 20
        ),
        name="main",
    )(top, bottom, west, east, patch_weight, conv_weight, bias, queries, here, left, right, kv_weight)


def read_stats(packed):
    def lanes(start):
        return packed if start == 0 else pltpu.roll(packed, 128 - start, 1)

    return (lanes(0) + lanes(8)) + lanes(16), lanes(24) + lanes(32)


def spread(factor):
    high = factor.astype(BF16)
    low = (factor - high.astype(F32)).astype(BF16)
    table = jnp.where(iota((256, 512), 0) % 128 == iota((256, 512), 1) // HEAD, 1.0, 0.0)
    return jnp.dot(
        jnp.concatenate([high, low], axis=1), table.astype(BF16), preferred_element_type=F32
    )


def pair_kernel(mine_ref, got_ref, out_ref):
    rows = LAT // 2
    lane = iota((rows, 128), 1)
    parts = []
    for half in range(2):
        here = slice(half * rows, (half + 1) * rows)
        peak_a, denom_a = read_stats(mine_ref[here, 512:640].astype(F32))
        peak_b, denom_b = read_stats(got_ref[here, 512:640].astype(F32))
        peak = jnp.maximum(peak_a, peak_b)
        factor_a = jnp.exp(peak_a - peak)
        factor_b = jnp.exp(peak_b - peak)
        sums = mine_ref[here, :512].astype(F32) * spread(factor_a) + got_ref[
            here, :512
        ].astype(F32) * spread(factor_b)
        denom = denom_a * factor_a + denom_b * factor_b
        high, middle, low = split3(jnp.where(lane < 8, peak, 0.0))
        above, below, _ = split3(jnp.where(lane < 8, denom, 0.0))
        packed = (
            high
            + pltpu.roll(middle, 8, 1)
            + pltpu.roll(low, 16, 1)
            + pltpu.roll(above, 24, 1)
            + pltpu.roll(below, 32, 1)
        )
        parts.append(jnp.concatenate([sums, packed], axis=1).reshape(rows // 8, 8, PART))
    first, second = parts
    upper = iota((rows // 8, 8, PART), 1) < 4
    even = jnp.where(upper, first, pltpu.roll(second, 4, 1))
    odd = jnp.where(upper, pltpu.roll(first, 4, 1), second)
    out_ref[...] = jnp.stack([even, odd], axis=1).reshape(LAT, PART).astype(BF16)


def pair(mine, got):
    return pl.pallas_call(
        pair_kernel,
        out_shape=jax.ShapeDtypeStruct((LAT, PART), BF16),
        compiler_params=params(),
        name="pair",
    )(mine, got)


def final_kernel(got_ref, weight_ref, out_ref):
    sources = got_ref.shape[0] // 8
    peak, denom = read_stats(got_ref[:, 512:640].astype(F32))
    peak = peak.reshape(sources, 8, 128)
    factor = jnp.exp(peak - jnp.max(peak, axis=0, keepdims=True))
    totals = jnp.sum(denom.reshape(sources, 8, 128) * factor, axis=0)
    sums = got_ref[:, :512].astype(F32) * spread(factor.reshape(sources * 8, 128))
    shares = jnp.sum(sums.reshape(sources, 8, 512), axis=0)
    lane = iota((8, 128), 1)
    attended = shares * spread(jnp.where(lane < 8, 1.0 / totals, 0.0))
    square = jnp.sum(attended * attended, axis=1, keepdims=True)
    square = (square + pltpu.roll(jnp.broadcast_to(square, (8, 128)), 4, 0)[:, :1]) / D
    normed = attended * lax.rsqrt(square + 1e-06)
    normed = jnp.concatenate([normed, pltpu.roll(normed, 4, 0)], axis=1).astype(BF16)
    result = jnp.dot(normed, weight_ref[...], preferred_element_type=F32)
    out_ref[...] = result[:OWN].astype(BF16)


def final(got, out_weight):
    return pl.pallas_call(
        final_kernel,
        out_shape=jax.ShapeDtypeStruct((OWN, D), BF16),
        compiler_params=params(),
        name="final",
    )(got, out_weight)


def neighbours(cells, axis):
    last, first = cells
    count = lax.axis_size(axis)
    up = [(i, i + 1) for i in range(count - 1)]
    down = [(i + 1, i) for i in range(count - 1)]
    return lax.ppermute(last, axis, up), lax.ppermute(first, axis, down)


def shards(pixels, tissue, patch_weight, conv_weight, kv_weight, query_weight, out_weight, latents):
    patch_in = pixels.shape[2]
    top, bottom = neighbours((pixels[TILE - 1], pixels[0]), "rows")
    west_edge = jnp.concatenate([top[:1], pixels[:, 0], bottom[:1]], axis=0)
    east_edge = jnp.concatenate([top[TILE - 1 :], pixels[:, TILE - 1], bottom[TILE - 1 :]], axis=0)
    west, east = neighbours((east_edge, west_edge), "cols")

    core = lax.axis_index("cols") % 2
    shifted = embed(pixels.reshape(TOK, patch_in), patch_weight)
    queries = make_queries(core.reshape(1).astype(jnp.int32), latents, query_weight)
    bias = jnp.broadcast_to(
        jnp.where(tissue.reshape(TOK, 1) > 0, 0.0, DEAD).astype(BF16), (TOK, 128)
    )
    features, mine, send = main(
        top, bottom, west, east, patch_weight, conv_weight, bias, queries, shifted, kv_weight
    )
    columns = lax.axis_size("cols")
    got = lax.ppermute(send, "cols", [(i, i ^ 1) for i in range(columns)])
    combined = pair(mine, got)
    chips = lax.axis_size(("rows", "cols")) // 2
    groups = [[2 * j + k for j in range(chips)] for k in range(2)]
    parts = lax.all_to_all(
        combined.reshape(chips, 8, PART),
        ("rows", "cols"),
        0,
        0,
        tiled=True,
        axis_index_groups=groups,
    )
    latents_out = final(parts.reshape(LAT, PART), out_weight)
    return features.reshape(TILE, TILE, D), latents_out


def solution(mesh):
    return jax.shard_map(
        shards,
        mesh=mesh,
        in_specs=(P("rows", "cols", None), P("rows", "cols"), P(), P(), P(), P(), P(), P()),
        out_specs=(P("rows", "cols", None), P(("rows", "cols"), None)),
        check_vma=False,
    )
```

```python
import functools

import jax
import jax.numpy as jnp
from jax import lax
from jax.experimental import pallas as pl
from jax.experimental.pallas import tpu as pltpu
from jax.sharding import PartitionSpec as P

HEADS = 16
HEAD = 64
D = 1024
TILE = 32
TOK = TILE * TILE
GW = 32
LAT = 512
OWN = 4
BLK = 256
CHUNK = 256
EMBED = 128
PART = 640
DEAD = -1e30
VMEM_BYTES = 56 * 1024 * 1024
F32 = jnp.float32
BF16 = jnp.bfloat16


def params():
    return pltpu.CompilerParams(vmem_limit_bytes=VMEM_BYTES)


def iota(shape, dim):
    return lax.broadcasted_iota(jnp.int32, shape, dim)


def query_kernel(latents_ref, weight_ref, tissue_ref, out_ref, bias_ref):
    core = lax.axis_index("cols") % 2
    row = iota((LAT, LAT), 0)
    inner = row % (LAT // 2)
    kind = jnp.where(row < LAT // 2, core, 1 - core)
    source = (inner // OWN) * (2 * OWN) + kind * OWN + inner % OWN
    pick = jnp.where(iota((LAT, LAT), 1) == source, 1.0, 0.0).astype(BF16)
    ordered = jnp.dot(pick, latents_ref[...], preferred_element_type=F32).astype(BF16)
    queries = jnp.dot(ordered, weight_ref[...], preferred_element_type=F32).astype(BF16)
    out_ref[...] = (queries.astype(F32) * HEAD ** (-0.5)).astype(BF16)
    none = jnp.where(tissue_ref[...] > 0, 0.0, 1.0).astype(BF16)
    pick_row = jnp.where(iota((TOK, TILE), 0) // TILE == iota((TOK, TILE), 1), 1.0, 0.0)
    by_row = jnp.dot(pick_row.astype(BF16), none, preferred_element_type=F32)
    own = jnp.where(iota((TOK, TILE), 0) % TILE == iota((TOK, TILE), 1), by_row, 0.0)
    flag = jnp.sum(own, axis=1, keepdims=True)
    bias_ref[...] = jnp.broadcast_to(flag * DEAD, (TOK, 128)).astype(BF16)


def make_queries(latents, query_weight, tissue):
    return pl.pallas_call(
        query_kernel,
        out_shape=[
            jax.ShapeDtypeStruct((LAT, D), BF16),
            jax.ShapeDtypeStruct((TOK, 128), BF16),
        ],
        compiler_params=params(),
        cost_estimate=pl.CostEstimate(
            flops=3 * LAT * D * D, bytes_accessed=4 << 20, transcendentals=0
        ),
        name="queries",
    )(latents, query_weight, tissue)


def split3(value):
    high = value.astype(BF16).astype(F32)
    rest = value - high
    middle = rest.astype(BF16).astype(F32)
    low = (rest - middle).astype(BF16).astype(F32)
    return high, middle, low


def main_kernel(
    top_ref,
    bottom_ref,
    west_ref,
    east_ref,
    conv_ref,
    pixels_hbm,
    patch_hbm,
    kv_hbm,
    query_hbm,
    bias_hbm,
    feat_hbm,
    mine_ref,
    send_ref,
    pixels,
    patch,
    kv,
    query_ref,
    bias_ref,
    cells,
    blocks,
    edges,
    summed,
    feats,
    proj,
    stats,
    sems,
    feat_sems,
):
    loads = [
        pltpu.make_async_copy(source, target, sems.at[n])
        for n, (source, target) in enumerate(
            (
                (patch_hbm, patch),
                (pixels_hbm, pixels),
                (kv_hbm, kv),
                (query_hbm, query_ref),
                (bias_hbm, bias_ref),
            )
        )
    ]
    for load in loads:
        load.start()

    same = iota((BLK, BLK), 0) // GW == iota((BLK, BLK), 1) // GW
    for b in range(D // BLK):
        for tap in range(9):
            rows = conv_ref[tap, :, b * BLK : (b + 1) * BLK]
            tiled = jnp.concatenate([rows] * (BLK // GW), axis=0)
            blocks[b, tap * BLK : (tap + 1) * BLK, :] = jnp.where(same, tiled, jnp.zeros_like(tiled))

    loads[0].wait()
    loads[1].wait()

    row_at, col_at = lax.axis_index("rows"), lax.axis_index("cols")
    row_last, col_last = lax.axis_size("rows") - 1, lax.axis_size("cols") - 1
    above, below = row_at > 0, row_at < row_last
    line = iota((TILE + 2, D), 0)
    inside = ((line > 0) | above) & ((line < TILE + 1) | below)
    for side, ref, there in ((0, west_ref, col_at > 0), (1, east_ref, col_at < col_last)):
        border = jnp.dot(ref[...], patch[...], preferred_element_type=F32)
        edges[side] = jnp.where(inside & there, border, 0.0)
    line = iota((TILE, D), 0)
    for ref, at, corner, there in (
        (top_ref, 0, 0, above),
        (bottom_ref, TILE + TOK, TILE + 1, below),
    ):
        border = jnp.dot(ref[...], patch[...], preferred_element_type=F32)
        border = jnp.where(there & (line >= 0), border, 0.0)
        west = edges[0, corner : corner + 1, :]
        east = edges[1, corner : corner + 1, :]
        cells[1, at : at + TILE, :] = border.astype(BF16)
        cells[0, at : at + TILE, :] = jnp.where(
            line == 0, west, pltpu.roll(border, 1, 0)
        ).astype(BF16)
        cells[2, at : at + TILE, :] = jnp.where(
            line == TILE - 1, east, pltpu.roll(border, TILE - 1, 0)
        ).astype(BF16)

    def embed_step(i, carry):
        at = pl.multiple_of(i * EMBED, EMBED)
        here = jnp.dot(pixels[pl.ds(at, EMBED), :], patch[...], preferred_element_type=F32)
        before = pltpu.roll(here, 1, 0)
        after = pltpu.roll(here, EMBED - 1, 0)
        rows = EMBED // TILE
        for r in range(rows):
            part = slice(r * TILE, (r + 1) * TILE)
            to = pl.ds(pl.multiple_of(TILE + at + r * TILE, TILE), TILE)
            west = edges[0, pl.ds(i * rows + r + 1, 1), :]
            east = edges[1, pl.ds(i * rows + r + 1, 1), :]
            cells[1, to, :] = here[part].astype(BF16)
            cells[0, to, :] = jnp.where(line == 0, west, before[part]).astype(BF16)
            cells[2, to, :] = jnp.where(line == TILE - 1, east, after[part]).astype(BF16)
        return carry

    lax.fori_loop(0, TOK // EMBED, embed_step, 0)
    loads[2].wait()

    def chunk_step(i, carry):
        at = pl.multiple_of(i * CHUNK, CHUNK)
        for b in range(D // BLK):
            lanes = slice(b * BLK, (b + 1) * BLK)
            taps = [
                cells[dc, pl.ds(at + dr * TILE, CHUNK), lanes] for dr in range(3) for dc in range(3)
            ]
            convolved = jnp.dot(
                jnp.concatenate(taps, axis=1), blocks[b], preferred_element_type=F32
            )
            summed[:, lanes] = convolved + taps[4].astype(F32)
        u = summed[...]
        centred = u - jnp.mean(u, axis=1, keepdims=True)
        variance = jnp.mean(centred * centred, axis=1, keepdims=True)
        normal = (centred * lax.rsqrt(variance + 1e-05)).astype(BF16)
        feats[pl.ds(at, CHUNK), :] = normal
        pltpu.make_async_copy(
            feats.at[pl.ds(at, CHUNK)], feat_hbm.at[pl.ds(at, CHUNK)], feat_sems.at[i]
        ).start()
        proj[pl.ds(at, CHUNK), :] = jnp.dot(
            normal, kv[...], preferred_element_type=F32
        ).astype(BF16)
        return carry

    lax.fori_loop(0, TOK // CHUNK, chunk_step, 0)

    loads[3].wait()
    loads[4].wait()
    half_rows = LAT // 2
    lane = iota((half_rows, 128), 1)
    unit = jnp.where(lane == 0, 1.0, 0.0).astype(BF16)
    ones = jnp.ones((TOK, 128), BF16)
    stats[...] = jnp.zeros_like(stats)
    outs = (mine_ref, send_ref)

    def pair_step(p, carry):
        half = p // 4
        inner = p % 4
        keys = proj[:, pl.ds(pl.multiple_of(p * 128, 128), 128)]
        values = proj[:, pl.ds(pl.multiple_of(D + p * 128, 128), 128)]
        keys = jnp.concatenate([keys, bias_ref[...]], axis=1)
        values = jnp.concatenate([values, ones], axis=1)
        for part in range(2):
            query = query_ref[
                part * half_rows : (part + 1) * half_rows,
                pl.ds(pl.multiple_of(p * 128, 128), 128),
            ]
            sums = []
            stat = stats[part, half]
            for a in range(2):
                own = jnp.where(lane // HEAD == a, query, jnp.zeros_like(query))
                scores = lax.dot_general(
                    jnp.concatenate([own, unit], axis=1),
                    keys,
                    (((1,), (1,)), ((), ())),
                    preferred_element_type=F32,
                )
                peak = jnp.max(scores, axis=1, keepdims=True)
                weights = jnp.exp(scores - peak).astype(BF16)
                total = jnp.dot(weights, values, preferred_element_type=F32)
                sums.append(total[:, :128])
                stat = jnp.where(
                    lane % 8 == 2 * inner + a, jnp.where(lane < 24, peak, total[:, 128:]), stat
                )
            stats[part, half] = stat
            rows = pl.ds(pl.multiple_of(half * half_rows, half_rows), half_rows)
            outs[part][rows, pl.ds(pl.multiple_of(inner * 128, 128), 128)] = jnp.where(
                lane < HEAD, sums[0], sums[1]
            ).astype(BF16)
        return carry

    lax.fori_loop(0, HEADS // 2, pair_step, 0)

    for part in range(2):
        for half in range(2):
            high, middle, low = split3(stats[part, half])
            packed = jnp.where(
                lane < 8,
                high,
                jnp.where(
                    lane < 16,
                    middle,
                    jnp.where(
                        lane < 24,
                        low,
                        jnp.where(lane < 32, high, jnp.where(lane < 40, middle, 0.0)),
                    ),
                ),
            )
            outs[part][half * half_rows : (half + 1) * half_rows, 512:640] = packed.astype(BF16)

    for i in range(TOK // CHUNK):
        pltpu.make_async_copy(
            feats.at[pl.ds(i * CHUNK, CHUNK)], feat_hbm.at[pl.ds(i * CHUNK, CHUNK)], feat_sems.at[i]
        ).wait()


def main(top, bottom, west, east, conv_weight, pixels, patch_weight, kv_weight, queries, bias):
    vmem = pl.BlockSpec(memory_space=pltpu.VMEM)
    hbm = pl.BlockSpec(memory_space=pl.ANY)
    return pl.pallas_call(
        main_kernel,
        in_specs=[vmem] * 5 + [hbm] * 5,
        out_specs=[hbm, vmem, vmem],
        out_shape=[
            jax.ShapeDtypeStruct((TOK, D), BF16),
            jax.ShapeDtypeStruct((LAT, PART), BF16),
            jax.ShapeDtypeStruct((LAT, PART), BF16),
        ],
        scratch_shapes=[
            pltpu.VMEM(pixels.shape, BF16),
            pltpu.VMEM(patch_weight.shape, BF16),
            pltpu.VMEM((D, 2 * D), BF16),
            pltpu.VMEM((LAT, D), BF16),
            pltpu.VMEM((TOK, 128), BF16),
            pltpu.VMEM((3, TOK + 2 * TILE, D), BF16),
            pltpu.VMEM((D // BLK, 9 * BLK, BLK), BF16),
            pltpu.VMEM((2, TILE + 2, D), F32),
            pltpu.VMEM((CHUNK, D), F32),
            pltpu.VMEM((TOK, D), BF16),
            pltpu.VMEM((TOK, 2 * D), BF16),
            pltpu.VMEM((2, 2, LAT // 2, 128), F32),
            pltpu.SemaphoreType.DMA((5,)),
            pltpu.SemaphoreType.DMA((TOK // CHUNK,)),
        ],
        compiler_params=params(),
        cost_estimate=pl.CostEstimate(
            flops=16 << 30, bytes_accessed=24 << 20, transcendentals=8 << 20
        ),
        name="main",
    )(top, bottom, west, east, conv_weight, pixels, patch_weight, kv_weight, queries, bias)


def read_stats(packed):
    def lanes(start):
        return packed if start == 0 else pltpu.roll(packed, 128 - start, 1)

    return (lanes(0) + lanes(8)) + lanes(16), lanes(24) + lanes(32)


def spread(factor):
    high = factor.astype(BF16)
    low = (factor - high.astype(F32)).astype(BF16)
    table = jnp.where(iota((256, 512), 0) % 128 == iota((256, 512), 1) // HEAD, 1.0, 0.0)
    return jnp.dot(
        jnp.concatenate([high, low], axis=1), table.astype(BF16), preferred_element_type=F32
    )


def pair_kernel(mine_ref, got_ref, out_ref):
    rows = LAT // 2
    lane = iota((rows, 128), 1)
    parts = []
    for half in range(2):
        here = slice(half * rows, (half + 1) * rows)
        peak_a, denom_a = read_stats(mine_ref[here, 512:640].astype(F32))
        peak_b, denom_b = read_stats(got_ref[here, 512:640].astype(F32))
        peak = jnp.maximum(peak_a, peak_b)
        factor_a = jnp.exp(peak_a - peak)
        factor_b = jnp.exp(peak_b - peak)
        sums = mine_ref[here, :512].astype(F32) * spread(factor_a) + got_ref[
            here, :512
        ].astype(F32) * spread(factor_b)
        denom = denom_a * factor_a + denom_b * factor_b
        high, middle, low = split3(jnp.where(lane < 8, peak, 0.0))
        above, below, _ = split3(jnp.where(lane < 8, denom, 0.0))
        packed = (
            high
            + pltpu.roll(middle, 8, 1)
            + pltpu.roll(low, 16, 1)
            + pltpu.roll(above, 24, 1)
            + pltpu.roll(below, 32, 1)
        )
        parts.append(jnp.concatenate([sums, packed], axis=1).reshape(rows // 8, 8, PART))
    first, second = parts
    upper = iota((rows // 8, 8, PART), 1) < 4
    even = jnp.where(upper, first, pltpu.roll(second, 4, 1))
    odd = jnp.where(upper, pltpu.roll(first, 4, 1), second)
    out_ref[...] = jnp.stack([even, odd], axis=1).reshape(LAT, PART).astype(BF16)


def pair(mine, got):
    return pl.pallas_call(
        pair_kernel,
        out_shape=jax.ShapeDtypeStruct((LAT, PART), BF16),
        compiler_params=params(),
        name="pair",
    )(mine, got)


def final_kernel(got_ref, weight_ref, out_ref):
    sources = got_ref.shape[0] // 8
    peak, denom = read_stats(got_ref[:, 512:640].astype(F32))
    peak = peak.reshape(sources, 8, 128)
    factor = jnp.exp(peak - jnp.max(peak, axis=0, keepdims=True))
    totals = jnp.sum(denom.reshape(sources, 8, 128) * factor, axis=0)
    sums = got_ref[:, :512].astype(F32) * spread(factor.reshape(sources * 8, 128))
    shares = jnp.sum(sums.reshape(sources, 8, 512), axis=0)
    lane = iota((8, 128), 1)
    attended = shares * spread(jnp.where(lane < 8, 1.0 / totals, 0.0))
    square = jnp.sum(attended * attended, axis=1, keepdims=True)
    square = (square + pltpu.roll(jnp.broadcast_to(square, (8, 128)), 4, 0)[:, :1]) / D
    normed = attended * lax.rsqrt(square + 1e-06)
    normed = jnp.concatenate([normed, pltpu.roll(normed, 4, 0)], axis=1).astype(BF16)
    result = jnp.dot(normed, weight_ref[...], preferred_element_type=F32)
    out_ref[...] = result[:OWN].astype(BF16)


def final(got, out_weight):
    return pl.pallas_call(
        final_kernel,
        out_shape=jax.ShapeDtypeStruct((OWN, D), BF16),
        compiler_params=params(),
        name="final",
    )(got, out_weight)


def neighbours(cells, axis):
    last, first = cells
    count = lax.axis_size(axis)
    up = [(i, (i + 1) % count) for i in range(count)]
    down = [((i + 1) % count, i) for i in range(count)]
    return lax.ppermute(last, axis, up), lax.ppermute(first, axis, down)


def shards(pixels, tissue, patch_weight, conv_weight, kv_weight, query_weight, out_weight, latents):
    patch_in = pixels.shape[2]
    top, bottom = neighbours((pixels[TILE - 1], pixels[0]), "rows")
    west_edge = jnp.concatenate([top[:1], pixels[:, 0], bottom[:1]], axis=0)
    east_edge = jnp.concatenate([top[TILE - 1 :], pixels[:, TILE - 1], bottom[TILE - 1 :]], axis=0)
    west, east = neighbours((east_edge, west_edge), "cols")

    queries, bias = make_queries(latents, query_weight, tissue)
    features, mine, send = main(
        top,
        bottom,
        west,
        east,
        conv_weight,
        pixels.reshape(TOK, patch_in),
        patch_weight,
        kv_weight,
        queries,
        bias,
    )
    columns = lax.axis_size("cols")
    got = lax.ppermute(send, "cols", [(i, i ^ 1) for i in range(columns)])
    combined = pair(mine, got)
    chips = lax.axis_size(("rows", "cols")) // 2
    groups = [[2 * j + k for j in range(chips)] for k in range(2)]
    parts = lax.all_to_all(
        combined.reshape(chips, 8, PART),
        ("rows", "cols"),
        0,
        0,
        tiled=True,
        axis_index_groups=groups,
    )
    latents_out = final(parts.reshape(LAT, PART), out_weight)
    return features.reshape(TILE, TILE, D), latents_out


def solution(mesh):
    return jax.shard_map(
        shards,
        mesh=mesh,
        in_specs=(P("rows", "cols", None), P("rows", "cols"), P(), P(), P(), P(), P(), P()),
        out_specs=(P("rows", "cols", None), P(("rows", "cols"), None)),
        check_vma=False,
    )
```

```python
import functools

import jax
import jax.numpy as jnp
from jax import lax
from jax.experimental import pallas as pl
from jax.experimental.pallas import tpu as pltpu
from jax.sharding import PartitionSpec as P

HEADS = 16
HEAD = 64
D = 1024
TILE = 32
TOK = TILE * TILE
PATCH_IN = 768
EDGE = 48
GW = 32
LAT = 512
OWN = 4
BLK = 256
CHUNK = 512
EMBED = 128
PART = 640
DEAD = -1e30
F32 = jnp.float32
BF16 = jnp.bfloat16


def params(mebibytes):
    return pltpu.CompilerParams(vmem_limit_bytes=mebibytes * 1024 * 1024)


def iota(shape, dim):
    return lax.broadcasted_iota(jnp.int32, shape, dim)


def query_kernel(latents_ref, weight_ref, tissue_ref, out_ref, bias_ref):
    core = lax.axis_index("cols") % 2
    row = iota((LAT, 1), 0)
    inner = row & (LAT // 2 - 1)
    kind = jnp.where(row < LAT // 2, core, 1 - core)
    source = ((inner >> 2) << 3) + kind * OWN + (inner & (OWN - 1))
    pick = jnp.where(iota((LAT, LAT), 1) == source, 1.0, 0.0).astype(BF16)
    ordered = jnp.dot(pick, latents_ref[...], preferred_element_type=F32).astype(BF16)
    queries = jnp.dot(ordered, weight_ref[...], preferred_element_type=F32).astype(BF16)
    out_ref[...] = (queries.astype(F32) * HEAD ** (-0.5)).astype(BF16)
    none = jnp.where(tissue_ref[...] > 0, 0.0, 1.0).astype(BF16)
    token, place = iota((TOK, TILE), 0), iota((TOK, TILE), 1)
    pick_row = jnp.where(token >> 5 == place, 1.0, 0.0)
    by_row = jnp.dot(pick_row.astype(BF16), none, preferred_element_type=F32)
    own = jnp.where(token & (TILE - 1) == place, by_row, 0.0).astype(BF16)
    flag = jnp.dot(own, jnp.full((TILE, 128), 1.0, BF16), preferred_element_type=F32)
    bias_ref[...] = (flag * DEAD).astype(BF16)


def make_queries(latents, query_weight, tissue):
    return pl.pallas_call(
        query_kernel,
        out_shape=[
            jax.ShapeDtypeStruct((LAT, D), BF16),
            jax.ShapeDtypeStruct((TOK, 128), BF16),
        ],
        compiler_params=params(16),
        cost_estimate=pl.CostEstimate(
            flops=3 * LAT * D * D, bytes_accessed=4 << 20, transcendentals=0
        ),
        name="queries",
    )(latents, query_weight, tissue)


def split3(value):
    high = value.astype(BF16).astype(F32)
    rest = value - high
    middle = rest.astype(BF16).astype(F32)
    low = (rest - middle).astype(BF16).astype(F32)
    return high, middle, low


def main_kernel(
    top_ref,
    bottom_ref,
    west_ref,
    east_ref,
    conv_ref,
    pixels,
    patch,
    kv,
    query_ref,
    bias_ref,
    feat_hbm,
    mine_ref,
    send_ref,
    cells,
    blocks,
    ring,
    edges,
    summed,
    feats,
    proj,
    stats,
    feat_sems,
):
    same = iota((BLK, BLK), 0) >> 5 == iota((BLK, BLK), 1) >> 5
    for b in range(D // BLK):
        for tap in range(9):
            rows = conv_ref[tap, :, b * BLK : (b + 1) * BLK]
            tiled = jnp.concatenate([rows] * (BLK // GW), axis=0)
            blocks[b, tap * BLK : (tap + 1) * BLK, :] = jnp.where(same, tiled, jnp.zeros_like(tiled))

    row_at, col_at = lax.axis_index("rows"), lax.axis_index("cols")
    row_last, col_last = lax.axis_size("rows") - 1, lax.axis_size("cols") - 1
    above, below = row_at > 0, row_at < row_last
    for at, ref in ((0, top_ref), (TILE, bottom_ref), (2 * TILE, west_ref), (2 * TILE + EDGE, east_ref)):
        ring[at : at + ref.shape[0], :] = ref[...]
    border = jnp.dot(ring[...], patch[...], preferred_element_type=F32)
    line = iota((EDGE, 1), 0)
    inside = ((line > 0) | above) & ((line < TILE + 1) | below)
    for side, there in ((0, col_at > 0), (1, col_at < col_last)):
        at = 2 * TILE + side * EDGE
        edges[side] = jnp.where(inside & there, border[at : at + EDGE], 0.0)
    line = iota((TILE, 1), 0)
    for part, at, corner, there in (
        (border[:TILE], 0, 0, above),
        (border[TILE : 2 * TILE], TILE + TOK, TILE + 1, below),
    ):
        part = jnp.where(there & (line >= 0), part, 0.0)
        west = edges[0, corner : corner + 1, :]
        east = edges[1, corner : corner + 1, :]
        cells[1, at : at + TILE, :] = part.astype(BF16)
        cells[0, at : at + TILE, :] = jnp.where(line == 0, west, pltpu.roll(part, 1, 0)).astype(
            BF16
        )
        cells[2, at : at + TILE, :] = jnp.where(
            line == TILE - 1, east, pltpu.roll(part, TILE - 1, 0)
        ).astype(BF16)

    def embed_step(i, carry):
        at = pl.multiple_of(i * EMBED, EMBED)
        here = jnp.dot(pixels[pl.ds(at, EMBED), :], patch[...], preferred_element_type=F32)
        before = pltpu.roll(here, 1, 0)
        after = pltpu.roll(here, EMBED - 1, 0)
        rows = EMBED // TILE
        for r in range(rows):
            part = slice(r * TILE, (r + 1) * TILE)
            to = pl.ds(pl.multiple_of(TILE + at + r * TILE, TILE), TILE)
            west = edges[0, pl.ds(i * rows + r + 1, 1), :]
            east = edges[1, pl.ds(i * rows + r + 1, 1), :]
            cells[1, to, :] = here[part].astype(BF16)
            cells[0, to, :] = jnp.where(line == 0, west, before[part]).astype(BF16)
            cells[2, to, :] = jnp.where(line == TILE - 1, east, after[part]).astype(BF16)
        return carry

    lax.fori_loop(0, TOK // EMBED, embed_step, 0)

    def chunk_step(i, carry):
        at = pl.multiple_of(i * CHUNK, CHUNK)
        for b in range(D // BLK):
            lanes = slice(b * BLK, (b + 1) * BLK)
            taps = [
                cells[dc, pl.ds(at + dr * TILE, CHUNK), lanes] for dr in range(3) for dc in range(3)
            ]
            convolved = jnp.dot(
                jnp.concatenate(taps, axis=1), blocks[b], preferred_element_type=F32
            )
            summed[:, lanes] = convolved + taps[4].astype(F32)
        u = summed[...]
        centred = u - jnp.mean(u, axis=1, keepdims=True)
        variance = jnp.mean(centred * centred, axis=1, keepdims=True)
        normal = (centred * lax.rsqrt(variance + 1e-05)).astype(BF16)
        feats[pl.ds(at, CHUNK), :] = normal
        pltpu.make_async_copy(
            feats.at[pl.ds(at, CHUNK)], feat_hbm.at[pl.ds(at, CHUNK)], feat_sems.at[i]
        ).start()

        proj[pl.ds(at, CHUNK), :] = jnp.dot(
            normal, kv[...], preferred_element_type=F32
        ).astype(BF16)
        return carry

    lax.fori_loop(0, TOK // CHUNK, chunk_step, 0)

    half_rows = LAT // 2
    lane = iota((half_rows, 128), 1)
    unit = jnp.where(lane == 0, 1.0, 0.0).astype(BF16)
    ones = jnp.ones((TOK, 128), BF16)
    stats[...] = jnp.zeros_like(stats)
    outs = (mine_ref, send_ref)

    def pair_step(p, carry):
        half = p // 4
        inner = p % 4
        keys = proj[:, pl.ds(pl.multiple_of(p * 128, 128), 128)]
        values = proj[:, pl.ds(pl.multiple_of(D + p * 128, 128), 128)]
        keys = jnp.concatenate([keys, bias_ref[...]], axis=1)
        values = jnp.concatenate([values, ones], axis=1)
        for part in range(2):
            query = query_ref[
                part * half_rows : (part + 1) * half_rows,
                pl.ds(pl.multiple_of(p * 128, 128), 128),
            ]
            sums = []
            stat = stats[part, half]
            for a in range(2):
                own = jnp.where(lane >> 6 == a, query, jnp.zeros_like(query))
                scores = lax.dot_general(
                    jnp.concatenate([own, unit], axis=1),
                    keys,
                    (((1,), (1,)), ((), ())),
                    preferred_element_type=F32,
                )
                peak = jnp.max(scores, axis=1, keepdims=True)
                weights = jnp.exp(scores - peak).astype(BF16)
                total = jnp.dot(weights, values, preferred_element_type=F32)
                sums.append(total[:, :128])
                stat = jnp.where(
                    lane & 7 == 2 * inner + a, jnp.where(lane < 24, peak, total[:, 128:]), stat
                )
            stats[part, half] = stat
            rows = pl.ds(pl.multiple_of(half * half_rows, half_rows), half_rows)
            outs[part][rows, pl.ds(pl.multiple_of(inner * 128, 128), 128)] = jnp.where(
                lane < HEAD, sums[0], sums[1]
            ).astype(BF16)
        return carry

    lax.fori_loop(0, HEADS // 2, pair_step, 0, unroll=2)

    for part in range(2):
        for half in range(2):
            high, middle, low = split3(stats[part, half])
            packed = jnp.where(
                lane < 8,
                high,
                jnp.where(
                    lane < 16,
                    middle,
                    jnp.where(
                        lane < 24,
                        low,
                        jnp.where(lane < 32, high, jnp.where(lane < 40, middle, 0.0)),
                    ),
                ),
            )
            outs[part][half * half_rows : (half + 1) * half_rows, 512:640] = packed.astype(BF16)

    for i in range(TOK // CHUNK):
        pltpu.make_async_copy(
            feats.at[pl.ds(i * CHUNK, CHUNK)], feat_hbm.at[pl.ds(i * CHUNK, CHUNK)], feat_sems.at[i]
        ).wait()


def main(top, bottom, west, east, conv_weight, pixels, patch_weight, kv_weight, queries, bias):
    vmem = pl.BlockSpec(memory_space=pltpu.VMEM)
    hbm = pl.BlockSpec(memory_space=pl.ANY)
    return pl.pallas_call(
        main_kernel,
        in_specs=[vmem] * 10,
        out_specs=[hbm, vmem, vmem],
        out_shape=[
            jax.ShapeDtypeStruct((TOK, D), BF16),
            jax.ShapeDtypeStruct((LAT, PART), BF16),
            jax.ShapeDtypeStruct((LAT, PART), BF16),
        ],
        scratch_shapes=[
            pltpu.VMEM((3, TOK + 2 * TILE, D), BF16),
            pltpu.VMEM((D // BLK, 9 * BLK, BLK), BF16),
            pltpu.VMEM((2 * TILE + 2 * EDGE, PATCH_IN), BF16),
            pltpu.VMEM((2, EDGE, D), F32),
            pltpu.VMEM((CHUNK, D), F32),
            pltpu.VMEM((TOK, D), BF16),
            pltpu.VMEM((TOK, 2 * D), BF16),
            pltpu.VMEM((2, 2, LAT // 2, 128), F32),
            pltpu.SemaphoreType.DMA((TOK // CHUNK,)),
        ],
        compiler_params=params(36),
        cost_estimate=pl.CostEstimate(
            flops=16 << 30, bytes_accessed=24 << 20, transcendentals=8 << 20
        ),
        name="main",
    )(top, bottom, west, east, conv_weight, pixels, patch_weight, kv_weight, queries, bias)


def read_stats(packed):
    def lanes(start):
        return packed if start == 0 else pltpu.roll(packed, 128 - start, 1)

    return (lanes(0) + lanes(8)) + lanes(16), lanes(24) + lanes(32)


def spread(factor):
    high = factor.astype(BF16)
    low = (factor - high.astype(F32)).astype(BF16)
    table = jnp.where(iota((256, 512), 0) & 127 == iota((256, 512), 1) >> 6, 1.0, 0.0)
    return jnp.dot(
        jnp.concatenate([high, low], axis=1), table.astype(BF16), preferred_element_type=F32
    )


def pair_kernel(mine_ref, got_ref, out_ref):
    rows = LAT // 2
    lane = iota((rows, 128), 1)
    parts = []
    for half in range(2):
        here = slice(half * rows, (half + 1) * rows)
        peak_a, denom_a = read_stats(mine_ref[here, 512:640].astype(F32))
        peak_b, denom_b = read_stats(got_ref[here, 512:640].astype(F32))
        peak = jnp.maximum(peak_a, peak_b)
        factor_a = jnp.exp(peak_a - peak)
        factor_b = jnp.exp(peak_b - peak)
        sums = mine_ref[here, :512].astype(F32) * spread(factor_a) + got_ref[
            here, :512
        ].astype(F32) * spread(factor_b)
        denom = denom_a * factor_a + denom_b * factor_b
        high, middle, low = split3(jnp.where(lane < 8, peak, 0.0))
        above, below, _ = split3(jnp.where(lane < 8, denom, 0.0))
        packed = (
            high
            + pltpu.roll(middle, 8, 1)
            + pltpu.roll(low, 16, 1)
            + pltpu.roll(above, 24, 1)
            + pltpu.roll(below, 32, 1)
        )
        parts.append(jnp.concatenate([sums, packed], axis=1).reshape(rows // 8, 8, PART))
    first, second = parts
    upper = iota((rows // 8, 8, PART), 1) < 4
    even = jnp.where(upper, first, pltpu.roll(second, 4, 1))
    odd = jnp.where(upper, pltpu.roll(first, 4, 1), second)
    out_ref[...] = jnp.stack([even, odd], axis=1).reshape(LAT, PART).astype(BF16)


def pair(mine, got):
    return pl.pallas_call(
        pair_kernel,
        out_shape=jax.ShapeDtypeStruct((LAT, PART), BF16),
        compiler_params=params(16),
        name="pair",
    )(mine, got)


def final_kernel(got_ref, weight_ref, out_ref):
    sources = got_ref.shape[0] // 8
    peak, denom = read_stats(got_ref[:, 512:640].astype(F32))
    peak = peak.reshape(sources, 8, 128)
    factor = jnp.exp(peak - jnp.max(peak, axis=0, keepdims=True))
    totals = jnp.sum(denom.reshape(sources, 8, 128) * factor, axis=0)
    sums = got_ref[:, :512].astype(F32) * spread(factor.reshape(sources * 8, 128))
    shares = jnp.sum(sums.reshape(sources, 8, 512), axis=0)
    lane = iota((8, 128), 1)
    attended = shares * spread(jnp.where(lane < 8, 1.0 / totals, 0.0))
    square = jnp.sum(attended * attended, axis=1, keepdims=True)
    square = (square + pltpu.roll(jnp.broadcast_to(square, (8, 128)), 4, 0)[:, :1]) / D
    normed = attended * lax.rsqrt(square + 1e-06)
    normed = jnp.concatenate([normed, pltpu.roll(normed, 4, 0)], axis=1).astype(BF16)
    result = jnp.dot(normed, weight_ref[...], preferred_element_type=F32)
    out_ref[...] = result[:OWN].astype(BF16)


def final(got, out_weight):
    return pl.pallas_call(
        final_kernel,
        out_shape=jax.ShapeDtypeStruct((OWN, D), BF16),
        compiler_params=params(16),
        name="final",
    )(got, out_weight)


def neighbours(cells, axis):
    last, first = cells
    count = lax.axis_size(axis)
    up = [(i, (i + 1) % count) for i in range(count)]
    down = [((i + 1) % count, i) for i in range(count)]
    return lax.ppermute(last, axis, up), lax.ppermute(first, axis, down)


def shards(pixels, tissue, patch_weight, conv_weight, kv_weight, query_weight, out_weight, latents):
    patch_in = pixels.shape[2]
    top, bottom = neighbours((pixels[TILE - 1], pixels[0]), "rows")
    spare = jnp.zeros((EDGE - TILE - 2, patch_in), BF16)
    west_edge = jnp.concatenate([top[:1], pixels[:, 0], bottom[:1], spare], axis=0)
    east_edge = jnp.concatenate(
        [top[TILE - 1 :], pixels[:, TILE - 1], bottom[TILE - 1 :], spare], axis=0
    )
    west, east = neighbours((east_edge, west_edge), "cols")

    queries, bias = make_queries(latents, query_weight, tissue)
    features, mine, send = main(
        top,
        bottom,
        west,
        east,
        conv_weight,
        pixels.reshape(TOK, patch_in),
        patch_weight,
        kv_weight,
        queries,
        bias,
    )
    columns = lax.axis_size("cols")
    got = lax.ppermute(send, "cols", [(i, i ^ 1) for i in range(columns)])
    combined = pair(mine, got)
    chips = lax.axis_size(("rows", "cols")) // 2
    groups = [[2 * j + k for j in range(chips)] for k in range(2)]
    parts = lax.all_to_all(
        combined.reshape(chips, 8, PART),
        ("rows", "cols"),
        0,
        0,
        tiled=True,
        axis_index_groups=groups,
    )
    latents_out = final(parts.reshape(LAT, PART), out_weight)
    return features.reshape(TILE, TILE, D), latents_out


def solution(mesh):
    return jax.shard_map(
        shards,
        mesh=mesh,
        in_specs=(P("rows", "cols", None), P("rows", "cols"), P(), P(), P(), P(), P(), P()),
        out_specs=(P("rows", "cols", None), P(("rows", "cols"), None)),
        check_vma=False,
    )
```

```python
import functools

import jax
import jax.numpy as jnp
from jax import lax
from jax.experimental import pallas as pl
from jax.experimental.pallas import tpu as pltpu
from jax.sharding import PartitionSpec as P

HEADS = 16
HEAD = 64
D = 1024
TILE = 32
TOK = TILE * TILE
PATCH_IN = 768
EDGE = 48
GW = 32
LAT = 512
OWN = 4
BLK = 256
CHUNK = 512
EMBED = 128
PART = 640
DEAD = -1e30
F32 = jnp.float32
BF16 = jnp.bfloat16


def params(mebibytes):
    return pltpu.CompilerParams(vmem_limit_bytes=mebibytes * 1024 * 1024)


def iota(shape, dim):
    return lax.broadcasted_iota(jnp.int32, shape, dim)


def query_kernel(
    latents_hbm,
    weight_hbm,
    patch_hbm,
    tissue_ref,
    out_ref,
    bias_ref,
    patch_ref,
    latents,
    weight,
    sems,
):
    loads = [
        pltpu.make_async_copy(latents_hbm, latents, sems.at[0]),
        pltpu.make_async_copy(weight_hbm, weight, sems.at[1]),
        pltpu.make_async_copy(patch_hbm, patch_ref, sems.at[2]),
    ]
    for load in loads:
        load.start()
    core = lax.axis_index("cols") % 2
    row = iota((LAT, 1), 0)
    inner = row & (LAT // 2 - 1)
    kind = jnp.where(row < LAT // 2, core, 1 - core)
    source = ((inner >> 2) << 3) + kind * OWN + (inner & (OWN - 1))
    pick = jnp.where(iota((LAT, LAT), 1) == source, 1.0, 0.0).astype(BF16)
    none = jnp.where(tissue_ref[...] > 0, 0.0, 1.0).astype(BF16)
    token, place = iota((TOK, TILE), 0), iota((TOK, TILE), 1)
    pick_row = jnp.where(token >> 5 == place, 1.0, 0.0)
    by_row = jnp.dot(pick_row.astype(BF16), none, preferred_element_type=F32)
    own = jnp.where(token & (TILE - 1) == place, by_row, 0.0).astype(BF16)
    flag = jnp.dot(own, jnp.full((TILE, 128), 1.0, BF16), preferred_element_type=F32)
    bias_ref[...] = (flag * DEAD).astype(BF16)
    loads[0].wait()
    ordered = jnp.dot(pick, latents[...], preferred_element_type=F32).astype(BF16)
    loads[1].wait()
    queries = jnp.dot(ordered, weight[...], preferred_element_type=F32).astype(BF16)
    out_ref[...] = (queries.astype(F32) * HEAD ** (-0.5)).astype(BF16)
    loads[2].wait()


def make_queries(latents, query_weight, patch_weight, tissue):
    hbm = pl.BlockSpec(memory_space=pltpu.HBM)
    return pl.pallas_call(
        query_kernel,
        in_specs=[hbm, hbm, hbm, pl.BlockSpec(memory_space=pltpu.VMEM)],
        out_shape=[
            jax.ShapeDtypeStruct((LAT, D), BF16),
            jax.ShapeDtypeStruct((TOK, 128), BF16),
            jax.ShapeDtypeStruct(patch_weight.shape, BF16),
        ],
        scratch_shapes=[
            pltpu.VMEM((LAT, D), BF16),
            pltpu.VMEM((D, D), BF16),
            pltpu.SemaphoreType.DMA((3,)),
        ],
        compiler_params=params(50),
        cost_estimate=pl.CostEstimate(
            flops=3 * LAT * D * D, bytes_accessed=4 << 20, transcendentals=0
        ),
        name="queries",
    )(latents, query_weight, patch_weight, tissue)


def split3(value):
    high = value.astype(BF16).astype(F32)
    rest = value - high
    middle = rest.astype(BF16).astype(F32)
    low = (rest - middle).astype(BF16).astype(F32)
    return high, middle, low


def main_kernel(
    top_ref,
    bottom_ref,
    west_ref,
    east_ref,
    conv_ref,
    pixels,
    patch,
    kv,
    query_ref,
    bias_ref,
    feat_hbm,
    mine_ref,
    send_ref,
    cells,
    blocks,
    ring,
    edges,
    summed,
    feats,
    proj,
    stats,
    feat_sems,
):
    same = iota((BLK, BLK), 0) >> 5 == iota((BLK, BLK), 1) >> 5
    for b in range(D // BLK):
        for tap in range(9):
            rows = conv_ref[tap, :, b * BLK : (b + 1) * BLK]
            tiled = jnp.concatenate([rows] * (BLK // GW), axis=0)
            blocks[b, tap * BLK : (tap + 1) * BLK, :] = jnp.where(same, tiled, jnp.zeros_like(tiled))

    row_at, col_at = lax.axis_index("rows"), lax.axis_index("cols")
    row_last, col_last = lax.axis_size("rows") - 1, lax.axis_size("cols") - 1
    above, below = row_at > 0, row_at < row_last
    for at, ref in ((0, top_ref), (TILE, bottom_ref), (2 * TILE, west_ref), (2 * TILE + EDGE, east_ref)):
        ring[at : at + ref.shape[0], :] = ref[...]
    border = jnp.dot(ring[...], patch[...], preferred_element_type=F32)
    line = iota((EDGE, 1), 0)
    inside = ((line > 0) | above) & ((line < TILE + 1) | below)
    for side, there in ((0, col_at > 0), (1, col_at < col_last)):
        at = 2 * TILE + side * EDGE
        edges[side] = jnp.where(inside & there, border[at : at + EDGE], 0.0)
    line = iota((TILE, 1), 0)
    for part, at, corner, there in (
        (border[:TILE], 0, 0, above),
        (border[TILE : 2 * TILE], TILE + TOK, TILE + 1, below),
    ):
        part = jnp.where(there & (line >= 0), part, 0.0)
        west = edges[0, corner : corner + 1, :]
        east = edges[1, corner : corner + 1, :]
        cells[1, at : at + TILE, :] = part.astype(BF16)
        cells[0, at : at + TILE, :] = jnp.where(line == 0, west, pltpu.roll(part, 1, 0)).astype(
            BF16
        )
        cells[2, at : at + TILE, :] = jnp.where(
            line == TILE - 1, east, pltpu.roll(part, TILE - 1, 0)
        ).astype(BF16)

    def embed_step(i, carry):
        at = pl.multiple_of(i * EMBED, EMBED)
        here = jnp.dot(pixels[pl.ds(at, EMBED), :], patch[...], preferred_element_type=F32)
        before = pltpu.roll(here, 1, 0)
        after = pltpu.roll(here, EMBED - 1, 0)
        rows = EMBED // TILE
        for r in range(rows):
            part = slice(r * TILE, (r + 1) * TILE)
            to = pl.ds(pl.multiple_of(TILE + at + r * TILE, TILE), TILE)
            west = edges[0, pl.ds(i * rows + r + 1, 1), :]
            east = edges[1, pl.ds(i * rows + r + 1, 1), :]
            cells[1, to, :] = here[part].astype(BF16)
            cells[0, to, :] = jnp.where(line == 0, west, before[part]).astype(BF16)
            cells[2, to, :] = jnp.where(line == TILE - 1, east, after[part]).astype(BF16)
        return carry

    lax.fori_loop(0, TOK // EMBED, embed_step, 0, unroll=True)

    def chunk_step(i, carry):
        at = pl.multiple_of(i * CHUNK, CHUNK)
        for b in range(D // BLK):
            lanes = slice(b * BLK, (b + 1) * BLK)
            taps = [
                cells[dc, pl.ds(at + dr * TILE, CHUNK), lanes] for dr in range(3) for dc in range(3)
            ]
            convolved = jnp.dot(
                jnp.concatenate(taps, axis=1), blocks[b], preferred_element_type=F32
            )
            summed[:, lanes] = convolved + taps[4].astype(F32)
        u = summed[...]
        centred = u - jnp.mean(u, axis=1, keepdims=True)
        variance = jnp.mean(centred * centred, axis=1, keepdims=True)
        normal = (centred * lax.rsqrt(variance + 1e-05)).astype(BF16)
        feats[pl.ds(at, CHUNK), :] = normal
        pltpu.make_async_copy(
            feats.at[pl.ds(at, CHUNK)], feat_hbm.at[pl.ds(at, CHUNK)], feat_sems.at[i]
        ).start()

        proj[pl.ds(at, CHUNK), :] = jnp.dot(
            normal, kv[...], preferred_element_type=F32
        ).astype(BF16)
        return carry

    lax.fori_loop(0, TOK // CHUNK, chunk_step, 0)

    half_rows = LAT // 2
    lane = iota((half_rows, 128), 1)
    unit = jnp.where(lane == 0, 1.0, 0.0).astype(BF16)
    ones = jnp.ones((TOK, 128), BF16)
    stats[...] = jnp.zeros_like(stats)
    outs = (mine_ref, send_ref)

    def pair_step(p, carry):
        half = p // 4
        inner = p % 4
        keys = proj[:, pl.ds(pl.multiple_of(p * 128, 128), 128)]
        values = proj[:, pl.ds(pl.multiple_of(D + p * 128, 128), 128)]
        keys = jnp.concatenate([keys, bias_ref[...]], axis=1)
        values = jnp.concatenate([values, ones], axis=1)
        for part in range(2):
            query = query_ref[
                part * half_rows : (part + 1) * half_rows,
                pl.ds(pl.multiple_of(p * 128, 128), 128),
            ]
            sums = []
            stat = stats[part, half]
            for a in range(2):
                own = jnp.where(lane >> 6 == a, query, jnp.zeros_like(query))
                scores = lax.dot_general(
                    jnp.concatenate([own, unit], axis=1),
                    keys,
                    (((1,), (1,)), ((), ())),
                    preferred_element_type=F32,
                )
                peak = jnp.max(scores, axis=1, keepdims=True)
                weights = jnp.exp(scores - peak).astype(BF16)
                total = jnp.dot(weights, values, preferred_element_type=F32)
                sums.append(total[:, :128])
                stat = jnp.where(
                    lane & 7 == 2 * inner + a, jnp.where(lane < 24, peak, total[:, 128:]), stat
                )
            stats[part, half] = stat
            rows = pl.ds(pl.multiple_of(half * half_rows, half_rows), half_rows)
            outs[part][rows, pl.ds(pl.multiple_of(inner * 128, 128), 128)] = jnp.where(
                lane < HEAD, sums[0], sums[1]
            ).astype(BF16)
        return carry

    lax.fori_loop(0, HEADS // 2, pair_step, 0, unroll=True)

    for part in range(2):
        for half in range(2):
            high, middle, low = split3(stats[part, half])
            packed = jnp.where(
                lane < 8,
                high,
                jnp.where(
                    lane < 16,
                    middle,
                    jnp.where(
                        lane < 24,
                        low,
                        jnp.where(lane < 32, high, jnp.where(lane < 40, middle, 0.0)),
                    ),
                ),
            )
            outs[part][half * half_rows : (half + 1) * half_rows, 512:640] = packed.astype(BF16)

    for i in range(TOK // CHUNK):
        pltpu.make_async_copy(
            feats.at[pl.ds(i * CHUNK, CHUNK)], feat_hbm.at[pl.ds(i * CHUNK, CHUNK)], feat_sems.at[i]
        ).wait()


def main(top, bottom, west, east, conv_weight, pixels, patch_weight, kv_weight, queries, bias):
    vmem = pl.BlockSpec(memory_space=pltpu.VMEM)
    hbm = pl.BlockSpec(memory_space=pl.ANY)
    return pl.pallas_call(
        main_kernel,
        in_specs=[vmem] * 10,
        out_specs=[hbm, vmem, vmem],
        out_shape=[
            jax.ShapeDtypeStruct((TOK, D), BF16),
            jax.ShapeDtypeStruct((LAT, PART), BF16),
            jax.ShapeDtypeStruct((LAT, PART), BF16),
        ],
        scratch_shapes=[
            pltpu.VMEM((3, TOK + 2 * TILE, D), BF16),
            pltpu.VMEM((D // BLK, 9 * BLK, BLK), BF16),
            pltpu.VMEM((2 * TILE + 2 * EDGE, PATCH_IN), BF16),
            pltpu.VMEM((2, EDGE, D), F32),
            pltpu.VMEM((CHUNK, D), F32),
            pltpu.VMEM((TOK, D), BF16),
            pltpu.VMEM((TOK, 2 * D), BF16),
            pltpu.VMEM((2, 2, LAT // 2, 128), F32),
            pltpu.SemaphoreType.DMA((TOK // CHUNK,)),
        ],
        compiler_params=params(36),
        cost_estimate=pl.CostEstimate(
            flops=16 << 30, bytes_accessed=24 << 20, transcendentals=8 << 20
        ),
        name="main",
    )(top, bottom, west, east, conv_weight, pixels, patch_weight, kv_weight, queries, bias)


def read_stats(packed):
    def lanes(start):
        return packed if start == 0 else pltpu.roll(packed, 128 - start, 1)

    return (lanes(0) + lanes(8)) + lanes(16), lanes(24) + lanes(32)


def spread(factor):
    high = factor.astype(BF16)
    low = (factor - high.astype(F32)).astype(BF16)
    table = jnp.where(iota((256, 512), 0) & 127 == iota((256, 512), 1) >> 6, 1.0, 0.0)
    return jnp.dot(
        jnp.concatenate([high, low], axis=1), table.astype(BF16), preferred_element_type=F32
    )


def pair_kernel(mine_ref, got_ref, out_ref):
    rows = LAT // 2
    lane = iota((rows, 128), 1)
    parts = []
    for half in range(2):
        here = slice(half * rows, (half + 1) * rows)
        peak_a, denom_a = read_stats(mine_ref[here, 512:640].astype(F32))
        peak_b, denom_b = read_stats(got_ref[here, 512:640].astype(F32))
        peak = jnp.maximum(peak_a, peak_b)
        factor_a = jnp.exp(peak_a - peak)
        factor_b = jnp.exp(peak_b - peak)
        sums = mine_ref[here, :512].astype(F32) * spread(factor_a) + got_ref[
            here, :512
        ].astype(F32) * spread(factor_b)
        denom = denom_a * factor_a + denom_b * factor_b
        high, middle, low = split3(jnp.where(lane < 8, peak, 0.0))
        above, below, _ = split3(jnp.where(lane < 8, denom, 0.0))
        packed = (
            high
            + pltpu.roll(middle, 8, 1)
            + pltpu.roll(low, 16, 1)
            + pltpu.roll(above, 24, 1)
            + pltpu.roll(below, 32, 1)
        )
        parts.append(jnp.concatenate([sums, packed], axis=1).reshape(rows // 8, 8, PART))
    first, second = parts
    upper = iota((rows // 8, 8, PART), 1) < 4
    even = jnp.where(upper, first, pltpu.roll(second, 4, 1))
    odd = jnp.where(upper, pltpu.roll(first, 4, 1), second)
    out_ref[...] = jnp.stack([even, odd], axis=1).reshape(LAT, PART).astype(BF16)


def pair(mine, got):
    return pl.pallas_call(
        pair_kernel,
        out_shape=jax.ShapeDtypeStruct((LAT, PART), BF16),
        compiler_params=params(16),
        name="pair",
    )(mine, got)


def final_kernel(got_ref, weight_ref, out_ref):
    sources = got_ref.shape[0] // 8
    peak, denom = read_stats(got_ref[:, 512:640].astype(F32))
    peak = peak.reshape(sources, 8, 128)
    factor = jnp.exp(peak - jnp.max(peak, axis=0, keepdims=True))
    totals = jnp.sum(denom.reshape(sources, 8, 128) * factor, axis=0)
    sums = got_ref[:, :512].astype(F32) * spread(factor.reshape(sources * 8, 128))
    shares = jnp.sum(sums.reshape(sources, 8, 512), axis=0)
    lane = iota((8, 128), 1)
    attended = shares * spread(jnp.where(lane < 8, 1.0 / totals, 0.0))
    square = jnp.sum(attended * attended, axis=1, keepdims=True)
    square = (square + pltpu.roll(jnp.broadcast_to(square, (8, 128)), 4, 0)[:, :1]) / D
    normed = attended * lax.rsqrt(square + 1e-06)
    normed = jnp.concatenate([normed, pltpu.roll(normed, 4, 0)], axis=1).astype(BF16)
    result = jnp.dot(normed, weight_ref[...], preferred_element_type=F32)
    out_ref[...] = result[:OWN].astype(BF16)


def final(got, out_weight):
    return pl.pallas_call(
        final_kernel,
        out_shape=jax.ShapeDtypeStruct((OWN, D), BF16),
        compiler_params=params(16),
        name="final",
    )(got, out_weight)


def neighbours(cells, axis):
    last, first = cells
    count = lax.axis_size(axis)
    up = [(i, (i + 1) % count) for i in range(count)]
    down = [((i + 1) % count, i) for i in range(count)]
    return lax.ppermute(last, axis, up), lax.ppermute(first, axis, down)


def shards(pixels, tissue, patch_weight, conv_weight, kv_weight, query_weight, out_weight, latents):
    patch_in = pixels.shape[2]
    queries, bias, patch_weight = make_queries(latents, query_weight, patch_weight, tissue)
    top, bottom = neighbours((pixels[TILE - 1], pixels[0]), "rows")
    spare = jnp.zeros((EDGE - TILE - 2, patch_in), BF16)
    west_edge = jnp.concatenate([top[:1], pixels[:, 0], bottom[:1], spare], axis=0)
    east_edge = jnp.concatenate(
        [top[TILE - 1 :], pixels[:, TILE - 1], bottom[TILE - 1 :], spare], axis=0
    )
    west_edge, east_edge, queries, bias, patch_weight = lax.optimization_barrier(
        (west_edge, east_edge, queries, bias, patch_weight)
    )
    west, east = neighbours((east_edge, west_edge), "cols")

    features, mine, send = main(
        top,
        bottom,
        west,
        east,
        conv_weight,
        pixels.reshape(TOK, patch_in),
        patch_weight,
        kv_weight,
        queries,
        bias,
    )
    columns = lax.axis_size("cols")
    got = lax.ppermute(send, "cols", [(i, i ^ 1) for i in range(columns)])
    combined = pair(mine, got)
    chips = lax.axis_size(("rows", "cols")) // 2
    groups = [[2 * j + k for j in range(chips)] for k in range(2)]
    parts = lax.all_to_all(
        combined.reshape(chips, 8, PART),
        ("rows", "cols"),
        0,
        0,
        tiled=True,
        axis_index_groups=groups,
    )
    latents_out = final(parts.reshape(LAT, PART), out_weight)
    return features.reshape(TILE, TILE, D), latents_out


def solution(mesh):
    return jax.shard_map(
        shards,
        mesh=mesh,
        in_specs=(P("rows", "cols", None), P("rows", "cols"), P(), P(), P(), P(), P(), P()),
        out_specs=(P("rows", "cols", None), P(("rows", "cols"), None)),
        check_vma=False,
    )
```

```python
import functools

import jax
import jax.numpy as jnp
from jax import lax
from jax.experimental import pallas as pl
from jax.experimental.pallas import tpu as pltpu
from jax.sharding import PartitionSpec as P

HEADS = 16
HEAD = 64
D = 1024
TILE = 32
TOK = TILE * TILE
PATCH_IN = 768
EDGE = 48
GW = 32
LAT = 512
OWN = 4
BLK = 256
CHUNK = 512
EMBED = 128
PART = 640
DEAD = -1e30
F32 = jnp.float32
BF16 = jnp.bfloat16


def params(mebibytes):
    return pltpu.CompilerParams(vmem_limit_bytes=mebibytes * 1024 * 1024)


def iota(shape, dim):
    return lax.broadcasted_iota(jnp.int32, shape, dim)


def query_kernel(
    latents_hbm,
    weight_hbm,
    patch_hbm,
    out_ref,
    patch_ref,
    latents,
    weight,
    sems,
):
    loads = [
        pltpu.make_async_copy(latents_hbm, latents, sems.at[0]),
        pltpu.make_async_copy(weight_hbm, weight, sems.at[1]),
        pltpu.make_async_copy(patch_hbm, patch_ref, sems.at[2]),
    ]
    for load in loads:
        load.start()
    core = lax.axis_index("cols") % 2
    row = iota((LAT, 1), 0)
    inner = row & (LAT // 2 - 1)
    kind = jnp.where(row < LAT // 2, core, 1 - core)
    source = ((inner >> 2) << 3) + kind * OWN + (inner & (OWN - 1))
    pick = jnp.where(iota((LAT, LAT), 1) == source, 1.0, 0.0).astype(BF16)
    loads[0].wait()
    ordered = jnp.dot(pick, latents[...], preferred_element_type=F32).astype(BF16)
    loads[1].wait()
    queries = jnp.dot(ordered, weight[...], preferred_element_type=F32).astype(BF16)
    out_ref[...] = (queries.astype(F32) * HEAD ** (-0.5)).astype(BF16)
    loads[2].wait()


def make_queries(latents, query_weight, patch_weight):
    hbm = pl.BlockSpec(memory_space=pltpu.HBM)
    return pl.pallas_call(
        query_kernel,
        in_specs=[hbm, hbm, hbm],
        out_shape=[
            jax.ShapeDtypeStruct((LAT, D), BF16),
            jax.ShapeDtypeStruct(patch_weight.shape, BF16),
        ],
        scratch_shapes=[
            pltpu.VMEM((LAT, D), BF16),
            pltpu.VMEM((D, D), BF16),
            pltpu.SemaphoreType.DMA((3,)),
        ],
        compiler_params=params(50),
        cost_estimate=pl.CostEstimate(
            flops=3 * LAT * D * D, bytes_accessed=4 << 20, transcendentals=0
        ),
        name="queries",
    )(latents, query_weight, patch_weight)


def table_kernel(conv_ref, tissue_ref, blocks, bias_ref):
    same = iota((BLK, BLK), 0) >> 5 == iota((BLK, BLK), 1) >> 5
    for b in range(D // BLK):
        for tap in range(9):
            rows = conv_ref[tap, :, b * BLK : (b + 1) * BLK]
            tiled = jnp.concatenate([rows] * (BLK // GW), axis=0)
            blocks[b, tap * BLK : (tap + 1) * BLK, :] = jnp.where(same, tiled, jnp.zeros_like(tiled))
    none = jnp.where(tissue_ref[...] > 0, 0.0, 1.0).astype(BF16)
    token, place = iota((TOK, TILE), 0), iota((TOK, TILE), 1)
    pick_row = jnp.where(token >> 5 == place, 1.0, 0.0)
    by_row = jnp.dot(pick_row.astype(BF16), none, preferred_element_type=F32)
    own = jnp.where(token & (TILE - 1) == place, by_row, 0.0).astype(BF16)
    flag = jnp.dot(own, jnp.full((TILE, 128), 1.0, BF16), preferred_element_type=F32)
    bias_ref[...] = (flag * DEAD).astype(BF16)


def tables(conv_weight, tissue):
    return pl.pallas_call(
        table_kernel,
        out_shape=[
            jax.ShapeDtypeStruct((D // BLK, 9 * BLK, BLK), BF16),
            jax.ShapeDtypeStruct((TOK, 128), BF16),
        ],
        compiler_params=params(8),
        cost_estimate=pl.CostEstimate(
            flops=1 << 30, bytes_accessed=6 << 20, transcendentals=0
        ),
        name="tables",
    )(conv_weight, tissue)


def split3(value):
    high = value.astype(BF16).astype(F32)
    rest = value - high
    middle = rest.astype(BF16).astype(F32)
    low = (rest - middle).astype(BF16).astype(F32)
    return high, middle, low


def main_kernel(
    top_ref,
    bottom_ref,
    west_ref,
    east_ref,
    blocks,
    pixels,
    patch,
    kv,
    query_ref,
    bias_ref,
    feat_hbm,
    mine_ref,
    send_ref,
    cells,
    ring,
    edges,
    summed,
    feats,
    proj,
    stats,
    feat_sems,
):
    row_at, col_at = lax.axis_index("rows"), lax.axis_index("cols")
    row_last, col_last = lax.axis_size("rows") - 1, lax.axis_size("cols") - 1
    above, below = row_at > 0, row_at < row_last
    for at, ref in ((0, top_ref), (TILE, bottom_ref), (2 * TILE, west_ref), (2 * TILE + EDGE, east_ref)):
        ring[at : at + ref.shape[0], :] = ref[...]
    border = jnp.dot(ring[...], patch[...], preferred_element_type=F32)
    line = iota((EDGE, 1), 0)
    inside = ((line > 0) | above) & ((line < TILE + 1) | below)
    for side, there in ((0, col_at > 0), (1, col_at < col_last)):
        at = 2 * TILE + side * EDGE
        edges[side] = jnp.where(inside & there, border[at : at + EDGE], 0.0)
    line = iota((TILE, 1), 0)
    for part, at, corner, there in (
        (border[:TILE], 0, 0, above),
        (border[TILE : 2 * TILE], TILE + TOK, TILE + 1, below),
    ):
        part = jnp.where(there & (line >= 0), part, 0.0)
        west = edges[0, corner : corner + 1, :]
        east = edges[1, corner : corner + 1, :]
        cells[1, at : at + TILE, :] = part.astype(BF16)
        cells[0, at : at + TILE, :] = jnp.where(line == 0, west, pltpu.roll(part, 1, 0)).astype(
            BF16
        )
        cells[2, at : at + TILE, :] = jnp.where(
            line == TILE - 1, east, pltpu.roll(part, TILE - 1, 0)
        ).astype(BF16)

    def embed_step(i, carry):
        at = pl.multiple_of(i * EMBED, EMBED)
        here = jnp.dot(pixels[pl.ds(at, EMBED), :], patch[...], preferred_element_type=F32)
        before = pltpu.roll(here, 1, 0)
        after = pltpu.roll(here, EMBED - 1, 0)
        rows = EMBED // TILE
        for r in range(rows):
            part = slice(r * TILE, (r + 1) * TILE)
            to = pl.ds(pl.multiple_of(TILE + at + r * TILE, TILE), TILE)
            west = edges[0, pl.ds(i * rows + r + 1, 1), :]
            east = edges[1, pl.ds(i * rows + r + 1, 1), :]
            cells[1, to, :] = here[part].astype(BF16)
            cells[0, to, :] = jnp.where(line == 0, west, before[part]).astype(BF16)
            cells[2, to, :] = jnp.where(line == TILE - 1, east, after[part]).astype(BF16)
        return carry

    lax.fori_loop(0, TOK // EMBED, embed_step, 0, unroll=True)

    def chunk_step(i, carry):
        at = pl.multiple_of(i * CHUNK, CHUNK)
        for b in range(D // BLK):
            lanes = slice(b * BLK, (b + 1) * BLK)
            taps = [
                cells[dc, pl.ds(at + dr * TILE, CHUNK), lanes] for dr in range(3) for dc in range(3)
            ]
            convolved = jnp.dot(
                jnp.concatenate(taps, axis=1), blocks[b], preferred_element_type=F32
            )
            summed[:, lanes] = convolved + taps[4].astype(F32)
        u = summed[...]
        centred = u - jnp.mean(u, axis=1, keepdims=True)
        variance = jnp.mean(centred * centred, axis=1, keepdims=True)
        normal = (centred * lax.rsqrt(variance + 1e-05)).astype(BF16)
        feats[pl.ds(at, CHUNK), :] = normal
        pltpu.make_async_copy(
            feats.at[pl.ds(at, CHUNK)], feat_hbm.at[pl.ds(at, CHUNK)], feat_sems.at[i]
        ).start()

        proj[pl.ds(at, CHUNK), :] = jnp.dot(
            normal, kv[...], preferred_element_type=F32
        ).astype(BF16)
        return carry

    lax.fori_loop(0, TOK // CHUNK, chunk_step, 0)

    half_rows = LAT // 2
    lane = iota((half_rows, 128), 1)
    unit = jnp.where(lane == 0, 1.0, 0.0).astype(BF16)
    ones = jnp.ones((TOK, 128), BF16)
    stats[...] = jnp.zeros_like(stats)
    outs = (mine_ref, send_ref)

    def pair_step(p, carry):
        half = p // 4
        inner = p % 4
        keys = proj[:, pl.ds(pl.multiple_of(p * 128, 128), 128)]
        values = proj[:, pl.ds(pl.multiple_of(D + p * 128, 128), 128)]
        keys = jnp.concatenate([keys, bias_ref[...]], axis=1)
        values = jnp.concatenate([values, ones], axis=1)
        for part in range(2):
            query = query_ref[
                part * half_rows : (part + 1) * half_rows,
                pl.ds(pl.multiple_of(p * 128, 128), 128),
            ]
            sums = []
            stat = stats[part, half]
            for a in range(2):
                own = jnp.where(lane >> 6 == a, query, jnp.zeros_like(query))
                scores = lax.dot_general(
                    jnp.concatenate([own, unit], axis=1),
                    keys,
                    (((1,), (1,)), ((), ())),
                    preferred_element_type=F32,
                )
                peak = jnp.max(scores, axis=1, keepdims=True)
                weights = jnp.exp(scores - peak).astype(BF16)
                total = jnp.dot(weights, values, preferred_element_type=F32)
                sums.append(total[:, :128])
                stat = jnp.where(
                    lane & 7 == 2 * inner + a, jnp.where(lane < 24, peak, total[:, 128:]), stat
                )
            stats[part, half] = stat
            rows = pl.ds(pl.multiple_of(half * half_rows, half_rows), half_rows)
            outs[part][rows, pl.ds(pl.multiple_of(inner * 128, 128), 128)] = jnp.where(
                lane < HEAD, sums[0], sums[1]
            ).astype(BF16)
        return carry

    lax.fori_loop(0, HEADS // 2, pair_step, 0, unroll=True)

    for part in range(2):
        for half in range(2):
            high, middle, low = split3(stats[part, half])
            packed = jnp.where(
                lane < 8,
                high,
                jnp.where(
                    lane < 16,
                    middle,
                    jnp.where(
                        lane < 24,
                        low,
                        jnp.where(lane < 32, high, jnp.where(lane < 40, middle, 0.0)),
                    ),
                ),
            )
            outs[part][half * half_rows : (half + 1) * half_rows, 512:640] = packed.astype(BF16)

    for i in range(TOK // CHUNK):
        pltpu.make_async_copy(
            feats.at[pl.ds(i * CHUNK, CHUNK)], feat_hbm.at[pl.ds(i * CHUNK, CHUNK)], feat_sems.at[i]
        ).wait()


def main(top, bottom, west, east, blocks, pixels, patch_weight, kv_weight, queries, bias):
    vmem = pl.BlockSpec(memory_space=pltpu.VMEM)
    hbm = pl.BlockSpec(memory_space=pl.ANY)
    return pl.pallas_call(
        main_kernel,
        in_specs=[vmem] * 10,
        out_specs=[hbm, vmem, vmem],
        out_shape=[
            jax.ShapeDtypeStruct((TOK, D), BF16),
            jax.ShapeDtypeStruct((LAT, PART), BF16),
            jax.ShapeDtypeStruct((LAT, PART), BF16),
        ],
        scratch_shapes=[
            pltpu.VMEM((3, TOK + 2 * TILE, D), BF16),
            pltpu.VMEM((2 * TILE + 2 * EDGE, PATCH_IN), BF16),
            pltpu.VMEM((2, EDGE, D), F32),
            pltpu.VMEM((CHUNK, D), F32),
            pltpu.VMEM((TOK, D), BF16),
            pltpu.VMEM((TOK, 2 * D), BF16),
            pltpu.VMEM((2, 2, LAT // 2, 128), F32),
            pltpu.SemaphoreType.DMA((TOK // CHUNK,)),
        ],
        compiler_params=params(31),
        cost_estimate=pl.CostEstimate(
            flops=16 << 30, bytes_accessed=24 << 20, transcendentals=8 << 20
        ),
        name="main",
    )(top, bottom, west, east, blocks, pixels, patch_weight, kv_weight, queries, bias)


def read_stats(packed):
    def lanes(start):
        return packed if start == 0 else pltpu.roll(packed, 128 - start, 1)

    return (lanes(0) + lanes(8)) + lanes(16), lanes(24) + lanes(32)


def spread(factor):
    high = factor.astype(BF16)
    low = (factor - high.astype(F32)).astype(BF16)
    table = jnp.where(iota((256, 512), 0) & 127 == iota((256, 512), 1) >> 6, 1.0, 0.0)
    return jnp.dot(
        jnp.concatenate([high, low], axis=1), table.astype(BF16), preferred_element_type=F32
    )


def pair_kernel(mine_ref, got_ref, out_ref):
    rows = LAT // 2
    lane = iota((rows, 128), 1)
    parts = []
    for half in range(2):
        here = slice(half * rows, (half + 1) * rows)
        peak_a, denom_a = read_stats(mine_ref[here, 512:640].astype(F32))
        peak_b, denom_b = read_stats(got_ref[here, 512:640].astype(F32))
        peak = jnp.maximum(peak_a, peak_b)
        factor_a = jnp.exp(peak_a - peak)
        factor_b = jnp.exp(peak_b - peak)
        sums = mine_ref[here, :512].astype(F32) * spread(factor_a) + got_ref[
            here, :512
        ].astype(F32) * spread(factor_b)
        denom = denom_a * factor_a + denom_b * factor_b
        high, middle, low = split3(jnp.where(lane < 8, peak, 0.0))
        above, below, _ = split3(jnp.where(lane < 8, denom, 0.0))
        packed = (
            high
            + pltpu.roll(middle, 8, 1)
            + pltpu.roll(low, 16, 1)
            + pltpu.roll(above, 24, 1)
            + pltpu.roll(below, 32, 1)
        )
        parts.append(jnp.concatenate([sums, packed], axis=1).reshape(rows // 8, 8, PART))
    first, second = parts
    upper = iota((rows // 8, 8, PART), 1) < 4
    even = jnp.where(upper, first, pltpu.roll(second, 4, 1))
    odd = jnp.where(upper, pltpu.roll(first, 4, 1), second)
    out_ref[...] = jnp.stack([even, odd], axis=1).reshape(LAT, PART).astype(BF16)


def pair(mine, got):
    return pl.pallas_call(
        pair_kernel,
        out_shape=jax.ShapeDtypeStruct((LAT, PART), BF16),
        compiler_params=params(16),
        name="pair",
    )(mine, got)


def final_kernel(got_ref, weight_ref, out_ref):
    sources = got_ref.shape[0] // 8
    peak, denom = read_stats(got_ref[:, 512:640].astype(F32))
    peak = peak.reshape(sources, 8, 128)
    factor = jnp.exp(peak - jnp.max(peak, axis=0, keepdims=True))
    totals = jnp.sum(denom.reshape(sources, 8, 128) * factor, axis=0)
    sums = got_ref[:, :512].astype(F32) * spread(factor.reshape(sources * 8, 128))
    shares = jnp.sum(sums.reshape(sources, 8, 512), axis=0)
    lane = iota((8, 128), 1)
    attended = shares * spread(jnp.where(lane < 8, 1.0 / totals, 0.0))
    square = jnp.sum(attended * attended, axis=1, keepdims=True)
    square = (square + pltpu.roll(jnp.broadcast_to(square, (8, 128)), 4, 0)[:, :1]) / D
    normed = attended * lax.rsqrt(square + 1e-06)
    normed = jnp.concatenate([normed, pltpu.roll(normed, 4, 0)], axis=1).astype(BF16)
    result = jnp.dot(normed, weight_ref[...], preferred_element_type=F32)
    out_ref[...] = result[:OWN].astype(BF16)


def final(got, out_weight):
    return pl.pallas_call(
        final_kernel,
        out_shape=jax.ShapeDtypeStruct((OWN, D), BF16),
        compiler_params=params(16),
        name="final",
    )(got, out_weight)


def neighbours(cells, axis):
    last, first = cells
    count = lax.axis_size(axis)
    up = [(i, (i + 1) % count) for i in range(count)]
    down = [((i + 1) % count, i) for i in range(count)]
    return lax.ppermute(last, axis, up), lax.ppermute(first, axis, down)


def shards(pixels, tissue, patch_weight, conv_weight, kv_weight, query_weight, out_weight, latents):
    patch_in = pixels.shape[2]
    queries, patch_weight = make_queries(latents, query_weight, patch_weight)
    top, bottom = neighbours((pixels[TILE - 1], pixels[0]), "rows")
    spare = jnp.zeros((EDGE - TILE - 2, patch_in), BF16)
    west_edge = jnp.concatenate([top[:1], pixels[:, 0], bottom[:1], spare], axis=0)
    east_edge = jnp.concatenate(
        [top[TILE - 1 :], pixels[:, TILE - 1], bottom[TILE - 1 :], spare], axis=0
    )
    west_edge, east_edge, queries, patch_weight, tissue = lax.optimization_barrier(
        (west_edge, east_edge, queries, patch_weight, tissue)
    )
    west, east = neighbours((east_edge, west_edge), "cols")

    blocks, bias = tables(conv_weight, tissue)
    features, mine, send = main(
        top,
        bottom,
        west,
        east,
        blocks,
        pixels.reshape(TOK, patch_in),
        patch_weight,
        kv_weight,
        queries,
        bias,
    )
    columns = lax.axis_size("cols")
    got = lax.ppermute(send, "cols", [(i, i ^ 1) for i in range(columns)])
    combined = pair(mine, got)
    chips = lax.axis_size(("rows", "cols")) // 2
    groups = [[2 * j + k for j in range(chips)] for k in range(2)]
    parts = lax.all_to_all(
        combined.reshape(chips, 8, PART),
        ("rows", "cols"),
        0,
        0,
        tiled=True,
        axis_index_groups=groups,
    )
    latents_out = final(parts.reshape(LAT, PART), out_weight)
    return features.reshape(TILE, TILE, D), latents_out


def solution(mesh):
    return jax.shard_map(
        shards,
        mesh=mesh,
        in_specs=(P("rows", "cols", None), P("rows", "cols"), P(), P(), P(), P(), P(), P()),
        out_specs=(P("rows", "cols", None), P(("rows", "cols"), None)),
        check_vma=False,
    )
```

```python
import functools

import jax
import jax.numpy as jnp
from jax import lax
from jax.experimental import pallas as pl
from jax.experimental.pallas import tpu as pltpu
from jax.sharding import PartitionSpec as P

HEADS = 16
HEAD = 64
D = 1024
TILE = 32
TOK = TILE * TILE
PATCH_IN = 768
EDGE = 48
GW = 32
LAT = 512
OWN = 4
BLK = 256
CHUNK = 512
EMBED = 128
PART = 640
DEAD = -1e30
F32 = jnp.float32
BF16 = jnp.bfloat16


def params(mebibytes):
    return pltpu.CompilerParams(vmem_limit_bytes=mebibytes * 1024 * 1024)


def iota(shape, dim):
    return lax.broadcasted_iota(jnp.int32, shape, dim)


def query_kernel(
    latents_hbm,
    weight_hbm,
    out_ref,
    latents,
    weight,
    sems,
):
    loads = [
        pltpu.make_async_copy(latents_hbm, latents, sems.at[0]),
        pltpu.make_async_copy(weight_hbm, weight, sems.at[1]),
    ]
    for load in loads:
        load.start()
    core = lax.axis_index("cols") % 2
    row = iota((LAT, 1), 0)
    inner = row & (LAT // 2 - 1)
    kind = jnp.where(row < LAT // 2, core, 1 - core)
    source = ((inner >> 2) << 3) + kind * OWN + (inner & (OWN - 1))
    pick = jnp.where(iota((LAT, LAT), 1) == source, 1.0, 0.0).astype(BF16)
    loads[0].wait()
    ordered = jnp.dot(pick, latents[...], preferred_element_type=F32).astype(BF16)
    loads[1].wait()
    queries = jnp.dot(ordered, weight[...], preferred_element_type=F32).astype(BF16)
    out_ref[...] = (queries.astype(F32) * HEAD ** (-0.5)).astype(BF16)


def make_queries(latents, query_weight):
    hbm = pl.BlockSpec(memory_space=pltpu.HBM)
    return pl.pallas_call(
        query_kernel,
        in_specs=[hbm, hbm],
        out_shape=[
            jax.ShapeDtypeStruct((LAT, D), BF16),
        ],
        scratch_shapes=[
            pltpu.VMEM((LAT, D), BF16),
            pltpu.VMEM((D, D), BF16),
            pltpu.SemaphoreType.DMA((2,)),
        ],
        compiler_params=params(52),
        cost_estimate=pl.CostEstimate(
            flops=3 * LAT * D * D, bytes_accessed=4 << 20, transcendentals=0
        ),
        name="queries",
    )(latents, query_weight)


def table_kernel(conv_ref, tissue_ref, blocks, bias_ref):
    same = iota((BLK, BLK), 0) >> 5 == iota((BLK, BLK), 1) >> 5
    for b in range(D // BLK):
        for tap in range(9):
            rows = conv_ref[tap, :, b * BLK : (b + 1) * BLK]
            tiled = jnp.concatenate([rows] * (BLK // GW), axis=0)
            blocks[b, tap * BLK : (tap + 1) * BLK, :] = jnp.where(same, tiled, jnp.zeros_like(tiled))
    none = jnp.where(tissue_ref[...] > 0, 0.0, 1.0).astype(BF16)
    token, place = iota((TOK, TILE), 0), iota((TOK, TILE), 1)
    pick_row = jnp.where(token >> 5 == place, 1.0, 0.0)
    by_row = jnp.dot(pick_row.astype(BF16), none, preferred_element_type=F32)
    own = jnp.where(token & (TILE - 1) == place, by_row, 0.0).astype(BF16)
    flag = jnp.dot(own, jnp.full((TILE, 128), 1.0, BF16), preferred_element_type=F32)
    bias_ref[...] = (flag * DEAD).astype(BF16)


def tables(conv_weight, tissue):
    return pl.pallas_call(
        table_kernel,
        out_shape=[
            jax.ShapeDtypeStruct((D // BLK, 9 * BLK, BLK), BF16),
            jax.ShapeDtypeStruct((TOK, 128), BF16),
        ],
        compiler_params=params(8),
        cost_estimate=pl.CostEstimate(
            flops=1 << 30, bytes_accessed=6 << 20, transcendentals=0
        ),
        name="tables",
    )(conv_weight, tissue)


def split3(value):
    high = value.astype(BF16).astype(F32)
    rest = value - high
    middle = rest.astype(BF16).astype(F32)
    low = (rest - middle).astype(BF16).astype(F32)
    return high, middle, low


def main_kernel(
    top_ref,
    bottom_ref,
    west_ref,
    east_ref,
    blocks,
    pixels,
    patch,
    kv,
    query_ref,
    bias_ref,
    feat_hbm,
    mine_ref,
    send_ref,
    cells,
    ring,
    edges,
    summed,
    feats,
    proj,
    stats,
    feat_sems,
):
    row_at, col_at = lax.axis_index("rows"), lax.axis_index("cols")
    row_last, col_last = lax.axis_size("rows") - 1, lax.axis_size("cols") - 1
    above, below = row_at > 0, row_at < row_last
    for at, ref in ((0, top_ref), (TILE, bottom_ref), (2 * TILE, west_ref), (2 * TILE + EDGE, east_ref)):
        ring[at : at + ref.shape[0], :] = ref[...]
    border = jnp.dot(ring[...], patch[...], preferred_element_type=F32)
    line = iota((EDGE, 1), 0)
    inside = ((line > 0) | above) & ((line < TILE + 1) | below)
    for side, there in ((0, col_at > 0), (1, col_at < col_last)):
        at = 2 * TILE + side * EDGE
        edges[side] = jnp.where(inside & there, border[at : at + EDGE], 0.0)
    line = iota((TILE, 1), 0)
    for part, at, corner, there in (
        (border[:TILE], 0, 0, above),
        (border[TILE : 2 * TILE], TILE + TOK, TILE + 1, below),
    ):
        part = jnp.where(there & (line >= 0), part, 0.0)
        west = edges[0, corner : corner + 1, :]
        east = edges[1, corner : corner + 1, :]
        cells[1, at : at + TILE, :] = part.astype(BF16)
        cells[0, at : at + TILE, :] = jnp.where(line == 0, west, pltpu.roll(part, 1, 0)).astype(
            BF16
        )
        cells[2, at : at + TILE, :] = jnp.where(
            line == TILE - 1, east, pltpu.roll(part, TILE - 1, 0)
        ).astype(BF16)

    def embed_step(i, carry):
        at = pl.multiple_of(i * EMBED, EMBED)
        here = jnp.dot(pixels[pl.ds(at, EMBED), :], patch[...], preferred_element_type=F32)
        before = pltpu.roll(here, 1, 0)
        after = pltpu.roll(here, EMBED - 1, 0)
        rows = EMBED // TILE
        for r in range(rows):
            part = slice(r * TILE, (r + 1) * TILE)
            to = pl.ds(pl.multiple_of(TILE + at + r * TILE, TILE), TILE)
            west = edges[0, pl.ds(i * rows + r + 1, 1), :]
            east = edges[1, pl.ds(i * rows + r + 1, 1), :]
            cells[1, to, :] = here[part].astype(BF16)
            cells[0, to, :] = jnp.where(line == 0, west, before[part]).astype(BF16)
            cells[2, to, :] = jnp.where(line == TILE - 1, east, after[part]).astype(BF16)
        return carry

    lax.fori_loop(0, TOK // EMBED, embed_step, 0, unroll=True)

    def chunk_step(i, carry):
        at = pl.multiple_of(i * CHUNK, CHUNK)
        for b in range(D // BLK):
            lanes = slice(b * BLK, (b + 1) * BLK)
            taps = [
                cells[dc, pl.ds(at + dr * TILE, CHUNK), lanes] for dr in range(3) for dc in range(3)
            ]
            convolved = jnp.dot(
                jnp.concatenate(taps, axis=1), blocks[b], preferred_element_type=F32
            )
            summed[:, lanes] = convolved + taps[4].astype(F32)
        u = summed[...]
        centred = u - jnp.mean(u, axis=1, keepdims=True)
        variance = jnp.mean(centred * centred, axis=1, keepdims=True)
        normal = (centred * lax.rsqrt(variance + 1e-05)).astype(BF16)
        feats[pl.ds(at, CHUNK), :] = normal
        pltpu.make_async_copy(
            feats.at[pl.ds(at, CHUNK)], feat_hbm.at[pl.ds(at, CHUNK)], feat_sems.at[i]
        ).start()

        proj[pl.ds(at, CHUNK), :] = jnp.dot(
            normal, kv[...], preferred_element_type=F32
        ).astype(BF16)
        return carry

    lax.fori_loop(0, TOK // CHUNK, chunk_step, 0, unroll=True)

    half_rows = LAT // 2
    lane = iota((half_rows, 128), 1)
    unit = jnp.where(lane == 0, 1.0, 0.0).astype(BF16)
    ones = jnp.ones((TOK, 128), BF16)
    stats[...] = jnp.zeros_like(stats)
    outs = (mine_ref, send_ref)

    def pair_step(p, carry):
        half = p // 4
        inner = p % 4
        keys = proj[:, pl.ds(pl.multiple_of(p * 128, 128), 128)]
        values = proj[:, pl.ds(pl.multiple_of(D + p * 128, 128), 128)]
        keys = jnp.concatenate([keys, bias_ref[...]], axis=1)
        values = jnp.concatenate([values, ones], axis=1)
        for part in range(2):
            query = query_ref[
                part * half_rows : (part + 1) * half_rows,
                pl.ds(pl.multiple_of(p * 128, 128), 128),
            ]
            sums = []
            stat = stats[part, half]
            for a in range(2):
                own = jnp.where(lane >> 6 == a, query, jnp.zeros_like(query))
                scores = lax.dot_general(
                    jnp.concatenate([own, unit], axis=1),
                    keys,
                    (((1,), (1,)), ((), ())),
                    preferred_element_type=F32,
                )
                peak = jnp.max(scores, axis=1, keepdims=True)
                weights = jnp.exp(scores - peak).astype(BF16)
                total = jnp.dot(weights, values, preferred_element_type=F32)
                sums.append(total[:, :128])
                stat = jnp.where(
                    lane & 7 == 2 * inner + a, jnp.where(lane < 24, peak, total[:, 128:]), stat
                )
            stats[part, half] = stat
            rows = pl.ds(pl.multiple_of(half * half_rows, half_rows), half_rows)
            outs[part][rows, pl.ds(pl.multiple_of(inner * 128, 128), 128)] = jnp.where(
                lane < HEAD, sums[0], sums[1]
            ).astype(BF16)
        return carry

    lax.fori_loop(0, HEADS // 2, pair_step, 0, unroll=True)

    for part in range(2):
        for half in range(2):
            high, middle, low = split3(stats[part, half])
            packed = jnp.where(
                lane < 8,
                high,
                jnp.where(
                    lane < 16,
                    middle,
                    jnp.where(
                        lane < 24,
                        low,
                        jnp.where(lane < 32, high, jnp.where(lane < 40, middle, 0.0)),
                    ),
                ),
            )
            outs[part][half * half_rows : (half + 1) * half_rows, 512:640] = packed.astype(BF16)

    for i in range(TOK // CHUNK):
        pltpu.make_async_copy(
            feats.at[pl.ds(i * CHUNK, CHUNK)], feat_hbm.at[pl.ds(i * CHUNK, CHUNK)], feat_sems.at[i]
        ).wait()


def main(top, bottom, west, east, blocks, pixels, patch_weight, kv_weight, queries, bias):
    vmem = pl.BlockSpec(memory_space=pltpu.VMEM)
    hbm = pl.BlockSpec(memory_space=pl.ANY)
    return pl.pallas_call(
        main_kernel,
        in_specs=[vmem] * 10,
        out_specs=[hbm, vmem, vmem],
        out_shape=[
            jax.ShapeDtypeStruct((TOK, D), BF16),
            jax.ShapeDtypeStruct((LAT, PART), BF16),
            jax.ShapeDtypeStruct((LAT, PART), BF16),
        ],
        scratch_shapes=[
            pltpu.VMEM((3, TOK + 2 * TILE, D), BF16),
            pltpu.VMEM((2 * TILE + 2 * EDGE, PATCH_IN), BF16),
            pltpu.VMEM((2, EDGE, D), F32),
            pltpu.VMEM((CHUNK, D), F32),
            pltpu.VMEM((TOK, D), BF16),
            pltpu.VMEM((TOK, 2 * D), BF16),
            pltpu.VMEM((2, 2, LAT // 2, 128), F32),
            pltpu.SemaphoreType.DMA((TOK // CHUNK,)),
        ],
        compiler_params=params(31),
        cost_estimate=pl.CostEstimate(
            flops=16 << 30, bytes_accessed=24 << 20, transcendentals=8 << 20
        ),
        name="main",
    )(top, bottom, west, east, blocks, pixels, patch_weight, kv_weight, queries, bias)


def read_stats(packed):
    def lanes(start):
        return packed if start == 0 else pltpu.roll(packed, 128 - start, 1)

    return (lanes(0) + lanes(8)) + lanes(16), lanes(24) + lanes(32)


def spread(factor):
    high = factor.astype(BF16)
    low = (factor - high.astype(F32)).astype(BF16)
    table = jnp.where(iota((256, 512), 0) & 127 == iota((256, 512), 1) >> 6, 1.0, 0.0)
    return jnp.dot(
        jnp.concatenate([high, low], axis=1), table.astype(BF16), preferred_element_type=F32
    )


def pair_kernel(mine_ref, got_ref, out_ref):
    rows = LAT // 2
    lane = iota((rows, 128), 1)
    parts = []
    for half in range(2):
        here = slice(half * rows, (half + 1) * rows)
        peak_a, denom_a = read_stats(mine_ref[here, 512:640].astype(F32))
        peak_b, denom_b = read_stats(got_ref[here, 512:640].astype(F32))
        peak = jnp.maximum(peak_a, peak_b)
        factor_a = jnp.exp(peak_a - peak)
        factor_b = jnp.exp(peak_b - peak)
        sums = mine_ref[here, :512].astype(F32) * spread(factor_a) + got_ref[
            here, :512
        ].astype(F32) * spread(factor_b)
        denom = denom_a * factor_a + denom_b * factor_b
        high, middle, low = split3(jnp.where(lane < 8, peak, 0.0))
        above, below, _ = split3(jnp.where(lane < 8, denom, 0.0))
        packed = (
            high
            + pltpu.roll(middle, 8, 1)
            + pltpu.roll(low, 16, 1)
            + pltpu.roll(above, 24, 1)
            + pltpu.roll(below, 32, 1)
        )
        parts.append(jnp.concatenate([sums, packed], axis=1).reshape(rows // 8, 8, PART))
    first, second = parts
    upper = iota((rows // 8, 8, PART), 1) < 4
    even = jnp.where(upper, first, pltpu.roll(second, 4, 1))
    odd = jnp.where(upper, pltpu.roll(first, 4, 1), second)
    out_ref[...] = jnp.stack([even, odd], axis=1).reshape(LAT, PART).astype(BF16)


def pair(mine, got):
    return pl.pallas_call(
        pair_kernel,
        out_shape=jax.ShapeDtypeStruct((LAT, PART), BF16),
        compiler_params=params(16),
        name="pair",
    )(mine, got)


def final_kernel(got_ref, weight_ref, out_ref):
    sources = got_ref.shape[0] // 8
    peak, denom = read_stats(got_ref[:, 512:640].astype(F32))
    peak = peak.reshape(sources, 8, 128)
    factor = jnp.exp(peak - jnp.max(peak, axis=0, keepdims=True))
    totals = jnp.sum(denom.reshape(sources, 8, 128) * factor, axis=0)
    sums = got_ref[:, :512].astype(F32) * spread(factor.reshape(sources * 8, 128))
    shares = jnp.sum(sums.reshape(sources, 8, 512), axis=0)
    lane = iota((8, 128), 1)
    attended = shares * spread(jnp.where(lane < 8, 1.0 / totals, 0.0))
    square = jnp.sum(attended * attended, axis=1, keepdims=True)
    square = (square + pltpu.roll(jnp.broadcast_to(square, (8, 128)), 4, 0)[:, :1]) / D
    normed = attended * lax.rsqrt(square + 1e-06)
    normed = jnp.concatenate([normed, pltpu.roll(normed, 4, 0)], axis=1).astype(BF16)
    result = jnp.dot(normed, weight_ref[...], preferred_element_type=F32)
    out_ref[...] = result[:OWN].astype(BF16)


def final(got, out_weight):
    return pl.pallas_call(
        final_kernel,
        out_shape=jax.ShapeDtypeStruct((OWN, D), BF16),
        compiler_params=params(16),
        name="final",
    )(got, out_weight)


def neighbours(cells, axis):
    last, first = cells
    count = lax.axis_size(axis)
    up = [(i, (i + 1) % count) for i in range(count)]
    down = [((i + 1) % count, i) for i in range(count)]
    return lax.ppermute(last, axis, up), lax.ppermute(first, axis, down)


def shards(pixels, tissue, patch_weight, conv_weight, kv_weight, query_weight, out_weight, latents):
    patch_in = pixels.shape[2]
    (queries,) = make_queries(latents, query_weight)
    top, bottom = neighbours((pixels[TILE - 1], pixels[0]), "rows")
    spare = jnp.zeros((EDGE - TILE - 2, patch_in), BF16)
    west_edge = jnp.concatenate([top[:1], pixels[:, 0], bottom[:1], spare], axis=0)
    east_edge = jnp.concatenate(
        [top[TILE - 1 :], pixels[:, TILE - 1], bottom[TILE - 1 :], spare], axis=0
    )
    west_edge, east_edge, queries, patch_weight, tissue = lax.optimization_barrier(
        (west_edge, east_edge, queries, patch_weight, tissue)
    )
    west, east = neighbours((east_edge, west_edge), "cols")

    blocks, bias = tables(conv_weight, tissue)
    features, mine, send = main(
        top,
        bottom,
        west,
        east,
        blocks,
        pixels.reshape(TOK, patch_in),
        patch_weight,
        kv_weight,
        queries,
        bias,
    )
    columns = lax.axis_size("cols")
    got = lax.ppermute(send, "cols", [(i, i ^ 1) for i in range(columns)])
    combined = pair(mine, got)
    chips = lax.axis_size(("rows", "cols")) // 2
    groups = [[2 * j + k for j in range(chips)] for k in range(2)]
    parts = lax.all_to_all(
        combined.reshape(chips, 8, PART),
        ("rows", "cols"),
        0,
        0,
        tiled=True,
        axis_index_groups=groups,
    )
    latents_out = final(parts.reshape(LAT, PART), out_weight)
    return features.reshape(TILE, TILE, D), latents_out


def solution(mesh):
    return jax.shard_map(
        shards,
        mesh=mesh,
        in_specs=(P("rows", "cols", None), P("rows", "cols"), P(), P(), P(), P(), P(), P()),
        out_specs=(P("rows", "cols", None), P(("rows", "cols"), None)),
        check_vma=False,
    )
```

```python
import functools

import jax
import jax.numpy as jnp
from jax import lax
from jax.experimental import pallas as pl
from jax.experimental.pallas import tpu as pltpu
from jax.sharding import PartitionSpec as P

HEADS = 16
HEAD = 64
D = 1024
TILE = 32
TOK = TILE * TILE
PATCH_IN = 768
EDGE = 48
GW = 32
LAT = 512
OWN = 4
BLK = 256
CHUNK = 512
EMBED = 128
PART = 640
DEAD = -1e30
F32 = jnp.float32
BF16 = jnp.bfloat16


def params(mebibytes):
    return pltpu.CompilerParams(vmem_limit_bytes=mebibytes * 1024 * 1024)


def iota(shape, dim):
    return lax.broadcasted_iota(jnp.int32, shape, dim)


def query_kernel(
    latents_hbm,
    weight_hbm,
    out_ref,
    latents,
    weight,
    sems,
):
    loads = [
        pltpu.make_async_copy(latents_hbm, latents, sems.at[0]),
        pltpu.make_async_copy(weight_hbm, weight, sems.at[1]),
    ]
    for load in loads:
        load.start()
    core = lax.axis_index("cols") % 2
    row = iota((LAT, 1), 0)
    inner = row & (LAT // 2 - 1)
    kind = jnp.where(row < LAT // 2, core, 1 - core)
    source = ((inner >> 2) << 3) + kind * OWN + (inner & (OWN - 1))
    pick = jnp.where(iota((LAT, LAT), 1) == source, 1.0, 0.0).astype(BF16)
    loads[0].wait()
    ordered = jnp.dot(pick, latents[...], preferred_element_type=F32).astype(BF16)
    loads[1].wait()
    queries = jnp.dot(ordered, weight[...], preferred_element_type=F32).astype(BF16)
    out_ref[...] = (queries.astype(F32) * HEAD ** (-0.5)).astype(BF16)


def make_queries(latents, query_weight):
    hbm = pl.BlockSpec(memory_space=pltpu.HBM)
    return pl.pallas_call(
        query_kernel,
        in_specs=[hbm, hbm],
        out_shape=[
            jax.ShapeDtypeStruct((LAT, D), BF16),
        ],
        scratch_shapes=[
            pltpu.VMEM((LAT, D), BF16),
            pltpu.VMEM((D, D), BF16),
            pltpu.SemaphoreType.DMA((2,)),
        ],
        compiler_params=params(52),
        cost_estimate=pl.CostEstimate(
            flops=3 * LAT * D * D, bytes_accessed=4 << 20, transcendentals=0
        ),
        name="queries",
    )(latents, query_weight)


def table_kernel(conv_ref, tissue_ref, blocks, bias_ref):
    same = iota((BLK, BLK), 0) >> 5 == iota((BLK, BLK), 1) >> 5
    for b in range(D // BLK):
        for tap in range(9):
            rows = conv_ref[tap, :, b * BLK : (b + 1) * BLK]
            tiled = jnp.concatenate([rows] * (BLK // GW), axis=0)
            blocks[b, tap * BLK : (tap + 1) * BLK, :] = jnp.where(same, tiled, jnp.zeros_like(tiled))
    none = jnp.where(tissue_ref[...] > 0, 0.0, 1.0).astype(BF16)
    token, place = iota((TOK, TILE), 0), iota((TOK, TILE), 1)
    pick_row = jnp.where(token >> 5 == place, 1.0, 0.0)
    by_row = jnp.dot(pick_row.astype(BF16), none, preferred_element_type=F32)
    own = jnp.where(token & (TILE - 1) == place, by_row, 0.0).astype(BF16)
    flag = jnp.dot(own, jnp.full((TILE, 128), 1.0, BF16), preferred_element_type=F32)
    bias_ref[...] = (flag * DEAD).astype(BF16)


def tables(conv_weight, tissue):
    return pl.pallas_call(
        table_kernel,
        out_shape=[
            jax.ShapeDtypeStruct((D // BLK, 9 * BLK, BLK), BF16),
            jax.ShapeDtypeStruct((TOK, 128), BF16),
        ],
        compiler_params=params(8),
        cost_estimate=pl.CostEstimate(
            flops=1 << 30, bytes_accessed=6 << 20, transcendentals=0
        ),
        name="tables",
    )(conv_weight, tissue)


def split3(value):
    high = value.astype(BF16).astype(F32)
    rest = value - high
    middle = rest.astype(BF16).astype(F32)
    low = (rest - middle).astype(BF16).astype(F32)
    return high, middle, low


def attend(part, query_ref, bias_ref, proj, stats, out_ref):
    half_rows = LAT // 2
    lane = iota((half_rows, 128), 1)
    unit = jnp.where(lane == 0, 1.0, 0.0).astype(BF16)
    ones = jnp.ones((TOK, 128), BF16)
    stats[...] = jnp.zeros_like(stats)

    def pair_step(p, carry):
        half = p // 4
        inner = p % 4
        keys = proj[:, pl.ds(pl.multiple_of(p * 128, 128), 128)]
        values = proj[:, pl.ds(pl.multiple_of(D + p * 128, 128), 128)]
        keys = jnp.concatenate([keys, bias_ref[...]], axis=1)
        values = jnp.concatenate([values, ones], axis=1)
        query = query_ref[
            part * half_rows : (part + 1) * half_rows,
            pl.ds(pl.multiple_of(p * 128, 128), 128),
        ]
        sums = []
        stat = stats[half]
        for a in range(2):
            own = jnp.where(lane >> 6 == a, query, jnp.zeros_like(query))
            scores = lax.dot_general(
                jnp.concatenate([own, unit], axis=1),
                keys,
                (((1,), (1,)), ((), ())),
                preferred_element_type=F32,
            )
            peak = jnp.max(scores, axis=1, keepdims=True)
            weights = jnp.exp(scores - peak).astype(BF16)
            total = jnp.dot(weights, values, preferred_element_type=F32)
            sums.append(total[:, :128])
            stat = jnp.where(
                lane & 7 == 2 * inner + a, jnp.where(lane < 24, peak, total[:, 128:]), stat
            )
        stats[half] = stat
        rows = pl.ds(pl.multiple_of(half * half_rows, half_rows), half_rows)
        out_ref[rows, pl.ds(pl.multiple_of(inner * 128, 128), 128)] = jnp.where(
            lane < HEAD, sums[0], sums[1]
        ).astype(BF16)
        return carry

    lax.fori_loop(0, HEADS // 2, pair_step, 0, unroll=True)

    for half in range(2):
        high, middle, low = split3(stats[half])
        packed = jnp.where(
            lane < 8,
            high,
            jnp.where(
                lane < 16,
                middle,
                jnp.where(
                    lane < 24,
                    low,
                    jnp.where(lane < 32, high, jnp.where(lane < 40, middle, 0.0)),
                ),
            ),
        )
        out_ref[half * half_rows : (half + 1) * half_rows, 512:640] = packed.astype(BF16)


def own_kernel(query_ref, bias_ref, proj, mine_ref, stats):
    attend(0, query_ref, bias_ref, proj, stats, mine_ref)


def main_kernel(
    top_ref,
    bottom_ref,
    west_ref,
    east_ref,
    blocks,
    pixels,
    patch,
    kv,
    query_ref,
    bias_ref,
    feat_hbm,
    send_ref,
    proj,
    cells,
    ring,
    edges,
    summed,
    feats,
    stats,
    feat_sems,
):
    row_at, col_at = lax.axis_index("rows"), lax.axis_index("cols")
    row_last, col_last = lax.axis_size("rows") - 1, lax.axis_size("cols") - 1
    above, below = row_at > 0, row_at < row_last
    for at, ref in ((0, top_ref), (TILE, bottom_ref), (2 * TILE, west_ref), (2 * TILE + EDGE, east_ref)):
        ring[at : at + ref.shape[0], :] = ref[...]
    border = jnp.dot(ring[...], patch[...], preferred_element_type=F32)
    line = iota((EDGE, 1), 0)
    inside = ((line > 0) | above) & ((line < TILE + 1) | below)
    for side, there in ((0, col_at > 0), (1, col_at < col_last)):
        at = 2 * TILE + side * EDGE
        edges[side] = jnp.where(inside & there, border[at : at + EDGE], 0.0)
    line = iota((TILE, 1), 0)
    for part, at, corner, there in (
        (border[:TILE], 0, 0, above),
        (border[TILE : 2 * TILE], TILE + TOK, TILE + 1, below),
    ):
        part = jnp.where(there & (line >= 0), part, 0.0)
        west = edges[0, corner : corner + 1, :]
        east = edges[1, corner : corner + 1, :]
        cells[1, at : at + TILE, :] = part.astype(BF16)
        cells[0, at : at + TILE, :] = jnp.where(line == 0, west, pltpu.roll(part, 1, 0)).astype(
            BF16
        )
        cells[2, at : at + TILE, :] = jnp.where(
            line == TILE - 1, east, pltpu.roll(part, TILE - 1, 0)
        ).astype(BF16)

    def embed_step(i, carry):
        at = pl.multiple_of(i * EMBED, EMBED)
        here = jnp.dot(pixels[pl.ds(at, EMBED), :], patch[...], preferred_element_type=F32)
        before = pltpu.roll(here, 1, 0)
        after = pltpu.roll(here, EMBED - 1, 0)
        rows = EMBED // TILE
        for r in range(rows):
            part = slice(r * TILE, (r + 1) * TILE)
            to = pl.ds(pl.multiple_of(TILE + at + r * TILE, TILE), TILE)
            west = edges[0, pl.ds(i * rows + r + 1, 1), :]
            east = edges[1, pl.ds(i * rows + r + 1, 1), :]
            cells[1, to, :] = here[part].astype(BF16)
            cells[0, to, :] = jnp.where(line == 0, west, before[part]).astype(BF16)
            cells[2, to, :] = jnp.where(line == TILE - 1, east, after[part]).astype(BF16)
        return carry

    lax.fori_loop(0, TOK // EMBED, embed_step, 0, unroll=True)

    def chunk_step(i, carry):
        at = pl.multiple_of(i * CHUNK, CHUNK)
        for b in range(D // BLK):
            lanes = slice(b * BLK, (b + 1) * BLK)
            taps = [
                cells[dc, pl.ds(at + dr * TILE, CHUNK), lanes] for dr in range(3) for dc in range(3)
            ]
            convolved = jnp.dot(
                jnp.concatenate(taps, axis=1), blocks[b], preferred_element_type=F32
            )
            summed[:, lanes] = convolved + taps[4].astype(F32)
        u = summed[...]
        centred = u - jnp.mean(u, axis=1, keepdims=True)
        variance = jnp.mean(centred * centred, axis=1, keepdims=True)
        normal = (centred * lax.rsqrt(variance + 1e-05)).astype(BF16)
        feats[pl.ds(at, CHUNK), :] = normal
        pltpu.make_async_copy(
            feats.at[pl.ds(at, CHUNK)], feat_hbm.at[pl.ds(at, CHUNK)], feat_sems.at[i]
        ).start()

        proj[pl.ds(at, CHUNK), :] = jnp.dot(
            normal, kv[...], preferred_element_type=F32
        ).astype(BF16)
        return carry

    lax.fori_loop(0, TOK // CHUNK, chunk_step, 0, unroll=True)

    attend(1, query_ref, bias_ref, proj, stats, send_ref)

    for i in range(TOK // CHUNK):
        pltpu.make_async_copy(
            feats.at[pl.ds(i * CHUNK, CHUNK)], feat_hbm.at[pl.ds(i * CHUNK, CHUNK)], feat_sems.at[i]
        ).wait()


def main(top, bottom, west, east, blocks, pixels, patch_weight, kv_weight, queries, bias):
    vmem = pl.BlockSpec(memory_space=pltpu.VMEM)
    hbm = pl.BlockSpec(memory_space=pl.ANY)
    return pl.pallas_call(
        main_kernel,
        in_specs=[vmem] * 10,
        out_specs=[hbm, vmem, vmem],
        out_shape=[
            jax.ShapeDtypeStruct((TOK, D), BF16),
            jax.ShapeDtypeStruct((LAT, PART), BF16),
            jax.ShapeDtypeStruct((TOK, 2 * D), BF16),
        ],
        scratch_shapes=[
            pltpu.VMEM((3, TOK + 2 * TILE, D), BF16),
            pltpu.VMEM((2 * TILE + 2 * EDGE, PATCH_IN), BF16),
            pltpu.VMEM((2, EDGE, D), F32),
            pltpu.VMEM((CHUNK, D), F32),
            pltpu.VMEM((TOK, D), BF16),
            pltpu.VMEM((2, LAT // 2, 128), F32),
            pltpu.SemaphoreType.DMA((TOK // CHUNK,)),
        ],
        compiler_params=params(28),
        cost_estimate=pl.CostEstimate(
            flops=16 << 30, bytes_accessed=24 << 20, transcendentals=8 << 20
        ),
        name="main",
    )(top, bottom, west, east, blocks, pixels, patch_weight, kv_weight, queries, bias)


def own(queries, bias, proj):
    return pl.pallas_call(
        own_kernel,
        out_shape=jax.ShapeDtypeStruct((LAT, PART), BF16),
        scratch_shapes=[pltpu.VMEM((2, LAT // 2, 128), F32)],
        compiler_params=params(24),
        cost_estimate=pl.CostEstimate(
            flops=5 << 30, bytes_accessed=6 << 20, transcendentals=4 << 20
        ),
        name="own",
    )(queries, bias, proj)


def read_stats(packed):
    def lanes(start):
        return packed if start == 0 else pltpu.roll(packed, 128 - start, 1)

    return (lanes(0) + lanes(8)) + lanes(16), lanes(24) + lanes(32)


def spread(factor):
    high = factor.astype(BF16)
    low = (factor - high.astype(F32)).astype(BF16)
    table = jnp.where(iota((256, 512), 0) & 127 == iota((256, 512), 1) >> 6, 1.0, 0.0)
    return jnp.dot(
        jnp.concatenate([high, low], axis=1), table.astype(BF16), preferred_element_type=F32
    )


def pair_kernel(mine_ref, got_ref, out_ref):
    rows = LAT // 2
    lane = iota((rows, 128), 1)
    parts = []
    for half in range(2):
        here = slice(half * rows, (half + 1) * rows)
        peak_a, denom_a = read_stats(mine_ref[here, 512:640].astype(F32))
        peak_b, denom_b = read_stats(got_ref[here, 512:640].astype(F32))
        peak = jnp.maximum(peak_a, peak_b)
        factor_a = jnp.exp(peak_a - peak)
        factor_b = jnp.exp(peak_b - peak)
        sums = mine_ref[here, :512].astype(F32) * spread(factor_a) + got_ref[
            here, :512
        ].astype(F32) * spread(factor_b)
        denom = denom_a * factor_a + denom_b * factor_b
        high, middle, low = split3(jnp.where(lane < 8, peak, 0.0))
        above, below, _ = split3(jnp.where(lane < 8, denom, 0.0))
        packed = (
            high
            + pltpu.roll(middle, 8, 1)
            + pltpu.roll(low, 16, 1)
            + pltpu.roll(above, 24, 1)
            + pltpu.roll(below, 32, 1)
        )
        parts.append(jnp.concatenate([sums, packed], axis=1).reshape(rows // 8, 8, PART))
    first, second = parts
    upper = iota((rows // 8, 8, PART), 1) < 4
    even = jnp.where(upper, first, pltpu.roll(second, 4, 1))
    odd = jnp.where(upper, pltpu.roll(first, 4, 1), second)
    out_ref[...] = jnp.stack([even, odd], axis=1).reshape(LAT, PART).astype(BF16)


def pair(mine, got):
    return pl.pallas_call(
        pair_kernel,
        out_shape=jax.ShapeDtypeStruct((LAT, PART), BF16),
        compiler_params=params(16),
        name="pair",
    )(mine, got)


def final_kernel(got_ref, weight_ref, out_ref):
    sources = got_ref.shape[0] // 8
    peak, denom = read_stats(got_ref[:, 512:640].astype(F32))
    peak = peak.reshape(sources, 8, 128)
    factor = jnp.exp(peak - jnp.max(peak, axis=0, keepdims=True))
    totals = jnp.sum(denom.reshape(sources, 8, 128) * factor, axis=0)
    sums = got_ref[:, :512].astype(F32) * spread(factor.reshape(sources * 8, 128))
    shares = jnp.sum(sums.reshape(sources, 8, 512), axis=0)
    lane = iota((8, 128), 1)
    attended = shares * spread(jnp.where(lane < 8, 1.0 / totals, 0.0))
    square = jnp.sum(attended * attended, axis=1, keepdims=True)
    square = (square + pltpu.roll(jnp.broadcast_to(square, (8, 128)), 4, 0)[:, :1]) / D
    normed = attended * lax.rsqrt(square + 1e-06)
    normed = jnp.concatenate([normed, pltpu.roll(normed, 4, 0)], axis=1).astype(BF16)
    result = jnp.dot(normed, weight_ref[...], preferred_element_type=F32)
    out_ref[...] = result[:OWN].astype(BF16)


def final(got, out_weight):
    return pl.pallas_call(
        final_kernel,
        out_shape=jax.ShapeDtypeStruct((OWN, D), BF16),
        compiler_params=params(16),
        name="final",
    )(got, out_weight)


def neighbours(cells, axis):
    last, first = cells
    count = lax.axis_size(axis)
    up = [(i, (i + 1) % count) for i in range(count)]
    down = [((i + 1) % count, i) for i in range(count)]
    return lax.ppermute(last, axis, up), lax.ppermute(first, axis, down)


def shards(pixels, tissue, patch_weight, conv_weight, kv_weight, query_weight, out_weight, latents):
    patch_in = pixels.shape[2]
    (queries,) = make_queries(latents, query_weight)
    top, bottom = neighbours((pixels[TILE - 1], pixels[0]), "rows")
    spare = jnp.zeros((EDGE - TILE - 2, patch_in), BF16)
    west_edge = jnp.concatenate([top[:1], pixels[:, 0], bottom[:1], spare], axis=0)
    east_edge = jnp.concatenate(
        [top[TILE - 1 :], pixels[:, TILE - 1], bottom[TILE - 1 :], spare], axis=0
    )
    west_edge, east_edge, queries, patch_weight, tissue = lax.optimization_barrier(
        (west_edge, east_edge, queries, patch_weight, tissue)
    )
    west, east = neighbours((east_edge, west_edge), "cols")

    blocks, bias = tables(conv_weight, tissue)
    features, send, proj = main(
        top,
        bottom,
        west,
        east,
        blocks,
        pixels.reshape(TOK, patch_in),
        patch_weight,
        kv_weight,
        queries,
        bias,
    )
    columns = lax.axis_size("cols")
    got = lax.ppermute(send, "cols", [(i, i ^ 1) for i in range(columns)])
    mine = own(queries, bias, proj)
    combined = pair(mine, got)
    chips = lax.axis_size(("rows", "cols")) // 2
    groups = [[2 * j + k for j in range(chips)] for k in range(2)]
    parts = lax.all_to_all(
        combined.reshape(chips, 8, PART),
        ("rows", "cols"),
        0,
        0,
        tiled=True,
        axis_index_groups=groups,
    )
    latents_out = final(parts.reshape(LAT, PART), out_weight)
    return features.reshape(TILE, TILE, D), latents_out


def solution(mesh):
    return jax.shard_map(
        shards,
        mesh=mesh,
        in_specs=(P("rows", "cols", None), P("rows", "cols"), P(), P(), P(), P(), P(), P()),
        out_specs=(P("rows", "cols", None), P(("rows", "cols"), None)),
        check_vma=False,
    )
```
